32 devices in a mesh: rep: 2 (over x), ep: 4 (over y, core), grp: 4 (over z).
Axes of the slice: x: 2, y: 2, z: 4, core: 2. Of those that a mesh axis runs over, the one named last changes fastest.
Arguments:
- tokens: bfloat16 [4096, 4096], P(('rep', 'ep'), 'grp'), parts along dimension 0, may hold values from -6 to 6
- proj_in: bfloat16 [1024, 4096], P('ep', 'grp'), may hold values from -0.09375 to 0.09375
- proj_out: bfloat16 [1024, 4096], P('ep', 'grp'), may hold values from -0.1875 to 0.1875
- expert_up: bfloat16 [16, 1024, 2688], P(('ep', 'grp')), may hold values from -0.1875 to 0.1875
- expert_down: bfloat16 [16, 2688, 1024], P(('ep', 'grp')), may hold values from -0.125 to 0.125
- expert_ids: int32 [4096, 6], P(('rep', 'ep')), parts along dimension 0, may hold values from 0 to 15, as said below
- weight_codes: int32 [4096, 6], P(('rep', 'ep')), parts along dimension 0, may hold values from 1 to 64
Outputs:
- mixed: bfloat16 [4096, 4096], P(('rep', 'ep'), 'grp'), parts along dimension 0
The draws below stay inside these ranges and needn't reach their ends.
There are 2 independent parts, one for each index of `rep`. The reference program is written for one: setup_inputs(seed, part) draws one part's arguments, and reference() takes and returns one part's arrays. A program takes and returns all parts, laid end to end along the dimension named above; an argument that names none is the same for every part. Nothing has to cross between parts.
Inputs may be any that keep to these rules, and one draw needn't show every extreme that they name: `expert_ids`: expert e belongs to group e % 4. Each token picks 6 distinct experts, two in each of 3 distinct groups. Within each aligned block of 128 tokens (the tokens of one device), every group is picked from by exactly 96 tokens, no expert is picked by more than 64 tokens, and in every block each group has an expert picked by exactly 64.
All inputs are finite; a program needn't handle non-finite values.
Results may differ from the reference program's by a relative error of at most 0.012.
Values may be sent and summed in bfloat16 or wider, within the bound.
No kernel may reach another device: no remote copies, remote signals or barrier semaphores. Data moves between devices by JAX's collectives and lax.ppermute only.
A program may use at most 64 MiB of HBM per device.

```python
import jax
import jax.numpy as jnp
from jax import lax

D = 4096
L = 1024
FF = 2688
GROUP_HITS = 3
PICKS = 6
TOK_DEV = 128
EXPERTS = 16
MOST = 64
TOKENS = 2048
N_EP = 4
N_GRP = 4


def group_labels(key):
    key_order, key_slots = jax.random.split(key)
    group_rows = TOK_DEV * GROUP_HITS // N_GRP
    order = jax.random.permutation(key_order, jnp.arange(N_EP, dtype=jnp.int32))
    rest = 2 * group_rows - MOST
    base = rest // (N_EP - 1)
    extra = rest % (N_EP - 1)
    ranks = jnp.arange(N_EP, dtype=jnp.int32)
    counts = jnp.where(ranks == 0, MOST, base + (ranks - 1 < extra).astype(jnp.int32)).astype(jnp.int32)
    labels = jnp.repeat(order, counts, total_repeat_length=2 * group_rows)
    slot_perm = jax.random.permutation(key_slots, jnp.arange(group_rows, dtype=jnp.int32))
    return (labels, slot_perm)


def block_ids(key):
    key_start, key_groups = jax.random.split(key)
    group_rows = TOK_DEV * GROUP_HITS // N_GRP
    starts = jax.random.permutation(key_start, jnp.arange(TOK_DEV, dtype=jnp.int32) % N_GRP)
    groups = (starts[:, None] + jnp.arange(GROUP_HITS, dtype=jnp.int32)[None, :]) % N_GRP
    hit = jnp.any(groups[:, :, None] == jnp.arange(N_GRP, dtype=jnp.int32), axis=1).astype(jnp.int32)
    rank_all = jnp.cumsum(hit, axis=0) - hit
    rank = jnp.take_along_axis(rank_all, groups, axis=1)
    labels, slot_perm = jax.vmap(group_labels)(jax.random.split(key_groups, N_GRP))
    slot = slot_perm[groups, rank]
    first = labels[groups, slot]
    second = labels[groups, slot + group_rows]
    members = jnp.stack([first, second], axis=2)
    ids = members * N_GRP + groups[:, :, None]
    return ids.reshape(TOK_DEV, 2 * GROUP_HITS).astype(jnp.int32)


def draw_expert_ids(key, part):
    blocks = TOKENS // TOK_DEV
    keys = jax.random.split(jax.random.fold_in(key, 7), blocks)
    return jax.vmap(block_ids)(keys).reshape(TOKENS, PICKS)


def plant(values, own_key, low, largest):
    longest = values.shape.index(max(values.shape))
    spots = []
    for shift in (0, 1):
        where = [jax.random.randint(jax.random.fold_in(own_key, axis), (), 0, length) for axis, length in enumerate(values.shape)]
        where[longest] = (where[longest] + shift) % values.shape[longest]
        spots.append(tuple(where))
    return values.at[spots[0]].set(low).at[spots[1]].set(largest)


def shard_levels(stream_key, dims, cuts, smallest, largest):
    level, own = 1.0, jax.random.fold_in(stream_key, 6)
    for position, shards_of in cuts:
        steps = jnp.exp(jax.random.uniform(jax.random.fold_in(own, position), (shards_of,), jnp.float32, smallest / len(cuts), largest / len(cuts)))
        level = level * jnp.repeat(steps, dims[position] // shards_of).reshape([-1 if axis == position else 1 for axis in range(len(dims))])
    return level


def gaussian(stream_key, shape, deviation, bound, cuts=(), kind=jnp.bfloat16):
    values = deviation * jax.random.normal(stream_key, shape, jnp.float32)
    if cuts:
        values = values * shard_levels(stream_key, shape, cuts, -0.22, 0.18)
    return jnp.clip(values, -bound, bound).astype(kind)


def setup_inputs(seed: int = 0, part: int = 0) -> dict:
    key_list = jax.random.split(jax.random.key(seed), 8)
    own_keys = jax.random.split(jax.random.fold_in(key_list[7], part), 8)
    return {
        "tokens": gaussian(own_keys[0], (TOKENS, D), 1.0, 6.0, ((0, 4), (1, 4))),
        "proj_in": gaussian(key_list[1], (L, D), D ** -0.5, 0.09375, ((0, 4), (1, 4))),
        "proj_out": gaussian(key_list[2], (L, D), L ** -0.5, 0.1875, ((0, 4), (1, 4))),
        "expert_up": gaussian(key_list[3], (EXPERTS, L, FF), L ** -0.5, 0.1875, ((0, 16),)),
        "expert_down": gaussian(key_list[4], (EXPERTS, FF, L), FF ** -0.5, 0.125, ((0, 16),)),
        "expert_ids": draw_expert_ids(jax.random.fold_in(jax.random.fold_in(key_list[7], part), 71), part),
        "weight_codes": plant(jax.random.randint(own_keys[6], (TOKENS, PICKS), 1, 65), jax.random.fold_in(own_keys[6], 1), 1, 64).astype(jnp.int32),
    }


def reference(tokens, proj_in, proj_out, expert_up, expert_down, expert_ids, weight_codes):
    codes = weight_codes.astype(jnp.float32)
    route_weights = codes / jnp.sum(codes, axis=1, keepdims=True)
    latent = lax.dot_general(tokens, proj_in, (((1,), (1,)), ((), ())), preferred_element_type=jnp.float32).astype(jnp.bfloat16)
    flat_ids = expert_ids.reshape(-1).astype(jnp.int32)
    order = jnp.argsort(flat_ids, stable=True).astype(jnp.int32)
    sorted_ids = flat_ids[order]
    source_rows = (order // PICKS).astype(jnp.int32)
    block_rows = 128
    block_count = (TOKENS * PICKS) // block_rows

    def one_block(block):
        start = (block * block_rows).astype(jnp.int32)
        ids_here = lax.dynamic_slice_in_dim(sorted_ids, start, block_rows, 0)
        rows_here = lax.dynamic_slice_in_dim(source_rows, start, block_rows, 0)
        inputs = latent[rows_here]

        def apply_one(expert, accum):
            up_here = lax.dynamic_index_in_dim(expert_up, expert, 0, keepdims=False)
            down_here = lax.dynamic_index_in_dim(expert_down, expert, 0, keepdims=False)
            hidden = jnp.dot(inputs, up_here, preferred_element_type=jnp.float32)
            hidden = jnp.square(jnp.maximum(hidden, 0.0)).astype(jnp.bfloat16)
            result = jnp.dot(hidden, down_here, preferred_element_type=jnp.float32).astype(jnp.bfloat16)
            return jnp.where((ids_here == expert)[:, None], result, accum)

        empty = jnp.zeros((block_rows, L), jnp.bfloat16)
        return lax.fori_loop(ids_here[0], ids_here[block_rows - 1] + 1, apply_one, empty)

    outputs = lax.map(one_block, jnp.arange(block_count, dtype=jnp.int32)).reshape(TOKENS * PICKS, L)
    placed = jnp.zeros((TOKENS * PICKS, L), jnp.bfloat16).at[order].set(outputs).reshape(TOKENS, PICKS, L)
    combined = jnp.sum(route_weights[:, :, None] * placed.astype(jnp.float32), axis=1).astype(jnp.bfloat16)
    return jnp.dot(combined, proj_out, preferred_element_type=jnp.float32).astype(jnp.bfloat16)
```

```python
import functools

import jax
import jax.numpy as jnp
from jax import lax
from jax.experimental import pallas as pl
from jax.experimental.pallas import tpu as pltpu
from jax.sharding import PartitionSpec as P

BF16, F32, I32 = jnp.bfloat16, jnp.float32, jnp.int32
VMEM_LIMIT = 56 * 2**20


def hop(x, axis, step):
    count = lax.axis_size(axis)
    return lax.ppermute(x, axis, [(i, i ^ step) for i in range(count)])


def xor_order(x, axis, me, count):
    bit = 1
    while bit < count:
        parts = jnp.split(x, count // bit, axis=axis)
        swapped = jnp.concatenate([parts[i ^ 1] for i in range(len(parts))], axis=axis)
        x = jnp.where((me & bit) != 0, swapped, x)
        bit *= 2
    return x


def call(kernel, me, operands, outs, scratch=(), flops=0):
    vmem = pl.BlockSpec(memory_space=pltpu.VMEM)
    moved = sum(o.size * o.dtype.itemsize for o in (*operands, *outs))
    return pl.pallas_call(
        kernel,
        out_shape=tuple(outs),
        in_specs=[pl.BlockSpec(memory_space=pltpu.SMEM)] + [vmem] * len(operands),
        out_specs=tuple(vmem for _ in outs),
        scratch_shapes=list(scratch),
        cost_estimate=pl.CostEstimate(flops=flops, bytes_accessed=moved, transcendentals=0),
        compiler_params=pltpu.CompilerParams(vmem_limit_bytes=VMEM_LIMIT),
    )(me, *operands)


def tiles(total, tile, body):
    whole = total // tile

    def step(i, carry):
        body(pl.multiple_of(i * tile, tile), tile)
        return carry

    if whole:
        lax.fori_loop(0, whole, step, 0)
    if total % tile:
        body(whole * tile, total % tile)


def partial_kernel(n_rows, me_ref, tokens_ref, *refs):
    n_blocks = len(refs) - 2 - n_rows
    rows, outs, (weights, product) = refs[:n_rows], refs[n_rows:-2], refs[-2:]
    high = rows[0].shape[0]
    core, grp = me_ref[0] & 1, me_ref[1]
    for q in range(n_rows):
        place = (q // 2) * 2 * high + (core ^ (q % 2)) * high
        weights[pl.ds(pl.multiple_of(place, high), high), :] = rows[q][...]

    def body(start, width):
        product[:, pl.ds(start, width)] = lax.dot_general(
            tokens_ref[...], weights[pl.ds(start, width), :], (((1,), (1,)), ((), ())), preferred_element_type=F32
        ).astype(BF16)

    tiles(product.shape[1], min(256, product.shape[1]), body)
    block = product.shape[0] // n_blocks
    for k, out in enumerate(outs):
        out[...] = product[pl.ds(pl.multiple_of((grp ^ k) * block, block), block), :]


def one_hot(codes, height):
    at = lax.broadcasted_iota(I32, (height, codes.shape[1]), 0)
    return jnp.where(at == codes, 1.0, 0.0).astype(BF16)


def dispatch_kernel(me_ref, ranks_ref, *refs):
    n = len(refs) // 2
    parts, outs = refs[:n], refs[n:]
    total = parts[0][...].astype(F32)
    for part in parts[1:]:
        total += part[...].astype(F32)
    latent = total.astype(BF16)
    for k, out in enumerate(outs):
        pick = one_hot(ranks_ref[k], out.shape[0])
        out[...] = jnp.dot(pick, latent, preferred_element_type=F32).astype(BF16)


def up_kernel(sources, slots, me_ref, slot_ref, *refs):
    n = len(sources)
    near, far, (up_ref, hidden_ref, placed) = refs[:n], refs[n : 2 * n], refs[2 * n :]
    pair = near[0].shape[1]
    chip = me_ref[0] // 2
    for i, r in enumerate(sources):
        pick = one_hot(slot_ref[r], slots)
        for j in range(up_ref.shape[0] // pair):
            part = near[i][...] if j == 0 else far[i][:, (j - 1) * pair : j * pair]
            column = pl.multiple_of((chip ^ (r // 2) ^ j) * pair, pair)
            placed[i * slots : (i + 1) * slots, pl.ds(column, pair)] = jnp.dot(
                pick, part, preferred_element_type=F32
            ).astype(BF16)

    def body(start, width):
        hidden = jnp.dot(placed[...], up_ref[:, pl.ds(start, width)], preferred_element_type=F32)
        hidden_ref[:, pl.ds(start, width)] = jnp.square(jnp.maximum(hidden, 0.0)).astype(BF16)

    tiles(hidden_ref.shape[1], 512, body)


def down_kernel(sources, slots, first, me_ref, slot_ref, weight_ref, hidden_ref, down_ref, *refs):
    outs, scaled = refs[:-1], refs[-1]
    picks = [one_hot(slot_ref[r], slots) for r in sources]
    scale = jnp.concatenate(
        [jnp.sum(pick.astype(F32) * weight_ref[r], axis=1, keepdims=True) for pick, r in zip(picks, sources)], axis=0
    )
    width = scaled.shape[1]
    result = jnp.dot(hidden_ref[...], down_ref[:, first : first + width], preferred_element_type=F32)
    scaled[...] = (result * scale).astype(BF16)
    for i, out in enumerate(outs):
        out[...] = lax.dot_general(
            picks[i], scaled[i * slots : (i + 1) * slots, :], (((0,), (0,)), ((), ())), preferred_element_type=F32
        ).astype(BF16)


def join_kernel(n_in, me_ref, *refs):
    parts, outs = refs[:n_in], refs[n_in:]
    height = outs[0].shape[0]
    for k, out in enumerate(outs):
        rows = slice(k * height, (k + 1) * height)
        total = parts[0][rows, :].astype(F32)
        for part in parts[1:]:
            total += part[rows, :].astype(F32)
        out[...] = total.astype(BF16)


def combine_kernel(me_ref, ranks_ref, *refs):
    parts, out = refs[:-1], refs[-1]
    total = jnp.zeros(out.shape, F32)
    for k, part in enumerate(parts):
        pick = one_hot(ranks_ref[k], part.shape[0])
        total += lax.dot_general(pick, part[...], (((0,), (0,)), ((), ())), preferred_element_type=F32)
    out[...] = total.astype(BF16)


def mixed_kernel(n_rows, halves, me_ref, *refs):
    rows, latents, (out_ref, weights, gathered) = refs[:n_rows], refs[n_rows:-3], refs[-3:]
    ep, grp = me_ref[0], me_ref[1]
    high = rows[0].shape[0]
    for q in range(n_rows):
        weights[pl.ds(pl.multiple_of((ep ^ q) * high, high), high), :] = rows[q][...]
    block, width = latents[0].shape
    for i, part in enumerate(latents):
        k, h = i // halves, i % halves
        place = pl.ds(pl.multiple_of((grp ^ k) * block, block), block)
        gathered[place, h * width : (h + 1) * width] = part[...]

    def body(start, size):
        out_ref[:, pl.ds(start, size)] = jnp.dot(
            gathered[...], weights[:, pl.ds(start, size)], preferred_element_type=F32
        ).astype(BF16)

    tiles(out_ref.shape[1], min(256, out_ref.shape[1]), body)


def spread_ep(x):
    count = lax.axis_size("ep")
    near = [x] + [hop(x, "ep", 2 * k) for k in range(1, count // 2)]
    out = []
    for part in near:
        out += [part, hop(part, "ep", 1)]
    return out


def per_device(tokens, proj_in, proj_out, expert_up, expert_down, expert_ids, weight_codes):
    n_ep, n_grp = lax.axis_size("ep"), lax.axis_size("grp")
    ep, grp = lax.axis_index("ep"), lax.axis_index("grp")
    experts = n_ep * n_grp
    picks = expert_ids.shape[1]
    block = tokens.shape[0] // n_grp
    width, wide = expert_up.shape[1], expert_up.shape[2]
    high, depth = proj_in.shape
    hits = block * (picks // 2) // n_grp
    cap = max(2, (4 * block * picks + 3 * experts - 1) // (3 * experts))
    slots, lines = n_grp * cap, n_grp * hits
    me = jnp.stack([ep, grp]).astype(I32)
    shape = jax.ShapeDtypeStruct

    meta_own = jnp.concatenate([expert_ids.T, weight_codes.T], axis=0)
    before = (jnp.arange(block)[:, None] < jnp.arange(block)[None, :]).astype(BF16)

    def rank_of(hit):
        return jnp.dot(hit.astype(BF16), before, preferred_element_type=F32).astype(I32)

    own = lax.dynamic_slice_in_dim(expert_ids.T, grp * block, block, 1)
    group_of = grp ^ jnp.arange(n_grp, dtype=I32)
    own_hit = jnp.any((own % n_grp)[None] == group_of[:, None, None], axis=1)
    ranks = jnp.where(own_hit, rank_of(own_hit), -1)[:, None, :]

    rows_in = spread_ep(proj_in)

    def partial(rows):
        columns = high * len(rows)
        return call(
            functools.partial(partial_kernel, len(rows)),
            me,
            [tokens, *rows],
            [shape((block, columns), BF16)] * n_grp,
            [pltpu.VMEM((columns, depth), BF16), pltpu.VMEM((tokens.shape[0], columns), BF16)],
            flops=2 * tokens.shape[0] * columns * depth,
        )

    def latents(rows):
        cut = partial(rows)
        arrived = [cut[0]] + [hop(cut[k], "grp", k) for k in range(1, n_grp)]
        columns = cut[0].shape[1]
        chosen = call(dispatch_kernel, me, [ranks, *arrived], [shape((hits, columns), BF16)] * n_grp)
        arrived = [chosen[0]] + [hop(chosen[k], "grp", k) for k in range(1, n_grp)]
        return spread_ep(jnp.concatenate(arrived, axis=0))

    near = latents(rows_in[:2])
    far = latents(rows_in[2:])

    meta = jnp.stack(spread_ep(meta_own)).reshape(n_ep, 2 * picks, n_grp, block)
    meta = xor_order(meta, 2, grp, n_grp)
    ids, codes = meta[:, :picks], meta[:, picks:].astype(F32)
    mine = ids == ep * n_grp + grp
    picked = jnp.any(mine, axis=1)
    weight = jnp.sum(jnp.where(mine, codes, 0.0), axis=1) / jnp.sum(codes, axis=1)
    hit = jnp.any(ids % n_grp == grp, axis=1)
    flat = (n_ep * n_grp, block)
    rank = jnp.where(hit, rank_of(hit.reshape(flat)).reshape(hit.shape), -1)
    slot = rank_of(picked.reshape(flat)).reshape(hit.shape) + cap * jnp.arange(n_grp, dtype=I32)[None, :, None]
    at = rank[:, :, None, :] == jnp.arange(hits, dtype=I32)[None, None, :, None]
    line_slot = jnp.sum(jnp.where(at & picked[:, :, None, :], slot[:, :, None, :] + 1, 0), axis=3) - 1
    line_weight = jnp.sum(jnp.where(at, weight[:, :, None, :], 0.0), axis=3)
    line_slot = line_slot.reshape(n_ep, 1, lines)
    line_weight = line_weight.reshape(n_ep, 1, lines)

    half = width // 2
    results = []
    for sources in (range(2), range(2, n_ep)):
        sources = list(sources)
        n = len(sources) * slots
        [hidden] = call(
            functools.partial(up_kernel, sources, slots),
            me,
            [line_slot, *[near[r] for r in sources], *[far[r] for r in sources], expert_up[0]],
            [shape((n, wide), BF16)],
            [pltpu.VMEM((n, width), BF16)],
            flops=2 * n * width * wide,
        )
        results.append(
            [
                call(
                    functools.partial(down_kernel, sources, slots, first),
                    me,
                    [line_slot, line_weight, hidden, expert_down[0]],
                    [shape((lines, half), BF16)] * len(sources),
                    [pltpu.VMEM((n, half), BF16)],
                    flops=2 * n * half * wide,
                )
                for first in (0, half)
            ]
        )

    rows_out = spread_ep(proj_out)
    gathered = []
    for h in range(2):
        local, remote = results[0][h], results[1][h]
        parts = [local[0], hop(local[1], "ep", 1)]
        for k in range(1, n_ep // 2):
            both = remote[2 * k - 2].astype(F32) + hop(remote[2 * k - 1], "ep", 1).astype(F32)
            parts.append(hop(both.astype(BF16), "ep", 2 * k))
        cut = call(functools.partial(join_kernel, len(parts)), me, parts, [shape((hits, half), BF16)] * n_grp)
        arrived = [cut[0]] + [hop(cut[k], "grp", k) for k in range(1, n_grp)]
        [latent_out] = call(combine_kernel, me, [ranks, *arrived], [shape((block, half), BF16)])
        blocks = {0: latent_out}
        for k in range(1, n_grp):
            low = k & -k
            blocks[k] = hop(blocks[k ^ low], "grp", low)
        gathered.append(blocks)
    pieces = [gathered[h][k] for k in range(n_grp) for h in range(2)]
    [mixed] = call(
        functools.partial(mixed_kernel, n_ep, 2),
        me,
        [*rows_out, *pieces],
        [shape((tokens.shape[0], depth), BF16)],
        [pltpu.VMEM((width, depth), BF16), pltpu.VMEM((tokens.shape[0], width), BF16)],
        flops=2 * tokens.shape[0] * width * depth,
    )
    return mixed


def solution(mesh):
    in_specs = (
        P(("rep", "ep"), "grp"),
        P("ep", "grp"),
        P("ep", "grp"),
        P(("ep", "grp"), None, None),
        P(("ep", "grp"), None, None),
        P(("rep", "ep"), None),
        P(("rep", "ep"), None),
    )
    out_specs = P(("rep", "ep"), "grp")
    return jax.shard_map(
        per_device, mesh=mesh, in_specs=in_specs, out_specs=out_specs, check_vma=False
    )
```

```python
import functools
import math

import jax
import jax.numpy as jnp
from jax import lax
from jax.experimental import pallas as pl
from jax.experimental.pallas import tpu as pltpu
from jax.sharding import PartitionSpec as P

BF16, F32, I32 = jnp.bfloat16, jnp.float32, jnp.int32


def hop(x, axis, step):
    count = lax.axis_size(axis)
    return lax.ppermute(x, axis, [(i, i ^ step) for i in range(count)])


def after(x, *earlier):
    return lax.optimization_barrier((x, *earlier))[0]


def call(kernel, me, operands, outs, scratch=(), flops=1, room=4):
    vmem = pl.BlockSpec(memory_space=pltpu.VMEM)
    def size(arrays):
        return sum(math.prod(x.shape) * jnp.dtype(x.dtype).itemsize for x in arrays)

    moved = size(operands) + size(outs)
    limit = min(56 * 2**20, moved + size(scratch) + room * 2**20)
    return pl.pallas_call(
        kernel,
        out_shape=tuple(outs),
        in_specs=[pl.BlockSpec(memory_space=pltpu.SMEM)] + [vmem] * len(operands),
        out_specs=tuple(vmem for _ in outs),
        scratch_shapes=list(scratch),
        cost_estimate=pl.CostEstimate(
            flops=flops, bytes_accessed=moved, transcendentals=0
        ),
        compiler_params=pltpu.CompilerParams(vmem_limit_bytes=limit),
    )(me, *operands)


def partial_kernel(n_rows, me_ref, tokens_ref, *refs):
    n_blocks = len(refs) - 2 - n_rows
    rows, outs, (weights, product) = refs[:n_rows], refs[n_rows:-2], refs[-2:]
    high = rows[0].shape[0]
    core, grp = me_ref[0] & 1, me_ref[1]
    for q in range(n_rows):
        place = pl.multiple_of((q // 2) * 2 * high + (core ^ (q % 2)) * high, high)
        weights[pl.ds(place, high), :] = rows[q][...]
    tile = min(256, product.shape[1])
    for start in range(0, product.shape[1], tile):
        product[:, start : start + tile] = lax.dot_general(
            tokens_ref[...], weights[start : start + tile, :], (((1,), (1,)), ((), ())), preferred_element_type=F32
        ).astype(BF16)
    block = product.shape[0] // n_blocks
    for k, out in enumerate(outs):
        out[...] = product[pl.ds(pl.multiple_of((grp ^ k) * block, block), block), :]


def one_hot(codes, height):
    at = lax.broadcasted_iota(I32, (height, codes.shape[1]), 0)
    return jnp.where(at == codes, 1.0, 0.0).astype(BF16)


def earlier(hits):
    n = hits.shape[1]
    before = lax.broadcasted_iota(I32, (n, n), 0) < lax.broadcasted_iota(I32, (n, n), 1)
    return jnp.dot(hits.astype(BF16), jnp.where(before, 1.0, 0.0).astype(BF16), preferred_element_type=F32)


def ranks_kernel(me_ref, ids_ref, out_ref):
    groups = out_ref.shape[0]
    block = out_ref.shape[2]
    ids = ids_ref[:, pl.ds(pl.multiple_of(me_ref[1] * block, block), block)] & (groups - 1)
    hits = jnp.concatenate(
        [jnp.max(jnp.where(ids == (me_ref[1] ^ k), 1.0, 0.0), axis=0, keepdims=True) for k in range(groups)], axis=0
    )
    ranks = jnp.where(hits > 0.0, earlier(hits), -1.0).astype(I32)
    for k in range(groups):
        out_ref[k] = ranks[k : k + 1, :]


def route_kernel(groups, picks, cap, me_ref, *refs):
    metas, slot_ref, weight_ref = refs[:-2], refs[-2], refs[-1]
    block = metas[0].shape[1] // groups
    lines = slot_ref.shape[2]
    hits, picked, weights = [], [], []
    expert = me_ref[0] * groups + me_ref[1]
    for meta in metas:
        for k in range(groups):
            place = pl.ds(pl.multiple_of((me_ref[1] ^ k) * block, block), block)
            ids, codes = meta[:picks, place], meta[picks:, place].astype(F32)
            mine = jnp.where(ids == expert, 1.0, 0.0)
            hits.append(jnp.max(jnp.where((ids & (groups - 1)) == me_ref[1], 1.0, 0.0), axis=0, keepdims=True))
            picked.append(jnp.max(mine, axis=0, keepdims=True))
            weights.append(
                jnp.sum(mine * codes, axis=0, keepdims=True) / jnp.sum(codes, axis=0, keepdims=True)
            )
    ranks = earlier(jnp.concatenate(hits, axis=0))
    slots = earlier(jnp.concatenate(picked, axis=0))
    for r in range(len(metas)):
        rows = range(r * groups, (r + 1) * groups)
        height = lines // groups
        line = jnp.concatenate(
            [jnp.where(hits[i] > 0.0, ranks[i : i + 1, :] + k * height, -1.0) for k, i in enumerate(rows)], axis=1
        ).astype(I32)
        slot = jnp.concatenate(
            [jnp.where(picked[i] > 0.0, slots[i : i + 1, :] + (k * cap + 1), 0.0) for k, i in enumerate(rows)], axis=1
        )
        weight = jnp.concatenate([weights[i] for i in rows], axis=1)
        at = jnp.where(lax.broadcasted_iota(I32, (lines, line.shape[1]), 0) == line, 1.0, 0.0)
        moved = lax.dot_general(
            jnp.concatenate([slot, weight], axis=0), at, (((1,), (1,)), ((), ())),
            precision=lax.Precision.HIGHEST, preferred_element_type=F32,
        )
        slot_ref[r] = moved[:1, :].astype(I32) - 1
        weight_ref[r] = moved[1:, :]


def dispatch_kernel(me_ref, ranks_ref, *refs):
    n = len(refs) // 2
    parts, outs = refs[:n], refs[n:]
    total = parts[0][...].astype(F32)
    for part in parts[1:]:
        total += part[...].astype(F32)
    latent = total.astype(BF16)
    for k, out in enumerate(outs):
        pick = one_hot(ranks_ref[k], out.shape[0])
        out[...] = jnp.dot(pick, latent, preferred_element_type=F32).astype(BF16)


def up_kernel(sources, slots, tile, me_ref, slot_ref, *refs):
    n = len(sources)
    near, far, (up_ref, hidden_ref, placed) = refs[:n], refs[n : 2 * n], refs[2 * n :]
    pair = near[0].shape[1]
    chip = me_ref[0] // 2
    for i, r in enumerate(sources):
        pick = one_hot(slot_ref[r], slots)
        for j in range(up_ref.shape[0] // pair):
            part = near[i][...] if j == 0 else far[i][:, (j - 1) * pair : j * pair]
            column = pl.multiple_of((chip ^ (r // 2) ^ j) * pair, pair)
            placed[i * slots : (i + 1) * slots, pl.ds(column, pair)] = jnp.dot(
                pick, part, preferred_element_type=F32
            ).astype(BF16)
    total = hidden_ref.shape[1]
    for start in range(0, total, tile):
        span = slice(start, min(start + tile, total))
        hidden = jnp.dot(placed[...], up_ref[:, span], preferred_element_type=F32)
        hidden_ref[:, span] = jnp.square(jnp.maximum(hidden, 0.0)).astype(BF16)


def down_kernel(sources, slots, tile, first, stride, me_ref, slot_ref, weight_ref, hidden_ref, down_ref, *refs):
    outs, picked, scaled = refs[:-2], refs[-2], refs[-1]
    picks = [one_hot(slot_ref[r], slots) for r in sources]
    scale = jnp.concatenate(
        [jnp.sum(pick.astype(F32) * weight_ref[r], axis=1, keepdims=True) for pick, r in zip(picks, sources)], axis=0
    )
    for i in range(len(sources)):
        at = (first + i * stride) * slots
        picked[i * slots : (i + 1) * slots, :] = hidden_ref[at : at + slots, :]
    for start in range(0, scaled.shape[1], tile):
        span = slice(start, start + tile)
        result = jnp.dot(picked[...], down_ref[:, span], preferred_element_type=F32)
        scaled[:, span] = (result * scale).astype(BF16)
        for i, out in enumerate(outs):
            out[:, span] = lax.dot_general(
                picks[i], scaled[i * slots : (i + 1) * slots, span], (((0,), (0,)), ((), ())), preferred_element_type=F32
            ).astype(BF16)


def add_kernel(me_ref, *refs):
    n = len(refs) // 4
    half = refs[0].shape[1] // 2
    for i in range(n):
        for h in range(2):
            span = slice(h * half, (h + 1) * half)
            refs[2 * n + 2 * i + h][...] = (
                refs[i][:, span].astype(F32) + refs[n + i][:, span].astype(F32)
            ).astype(BF16)


def join_kernel(n_in, h, me_ref, *refs):
    parts, outs = refs[:n_in], refs[n_in:]
    height, width = outs[0].shape
    for k, out in enumerate(outs):
        rows = slice(k * height, (k + 1) * height)
        total = jnp.zeros((height, width), F32)
        for part in parts:
            first = h * width if part.shape[1] > width else 0
            total += part[rows, first : first + width].astype(F32)
        out[...] = total.astype(BF16)


def combine_kernel(me_ref, ranks_ref, *refs):
    parts, out = refs[:-1], refs[-1]
    total = jnp.zeros(out.shape, F32)
    for k, part in enumerate(parts):
        pick = one_hot(ranks_ref[k], part.shape[0])
        total += lax.dot_general(pick, part[...], (((0,), (0,)), ((), ())), preferred_element_type=F32)
    out[...] = total.astype(BF16)


def rows_kernel(me_ref, *refs):
    rows, out_ref = refs[:-1], refs[-1]
    high = rows[0].shape[0]
    for q, row in enumerate(rows):
        out_ref[pl.ds(pl.multiple_of((me_ref[0] ^ q) * high, high), high), :] = row[...]


def mixed_kernel(h, me_ref, weights_ref, *refs):
    latents, out_ref, gathered = refs[: -2 - h], refs[-2], refs[-1]
    block, width = latents[0].shape
    for k, part in enumerate(latents):
        gathered[pl.ds(pl.multiple_of((me_ref[1] ^ k) * block, block), block), :] = part[...]
    tile = min(256, out_ref.shape[1])
    for start in range(0, out_ref.shape[1], tile):
        span = slice(start, start + tile)
        total = jnp.dot(
            gathered[...], weights_ref[h * width : (h + 1) * width, span], preferred_element_type=F32
        )
        if h:
            total += refs[-3][:, span]
        out_ref[:, span] = total.astype(out_ref.dtype)


def spread_ep(x):
    count = lax.axis_size("ep")
    near = [x] + [hop(x, "ep", 2 * k) for k in range(1, count // 2)]
    out = []
    for part in near:
        out += [part, hop(part, "ep", 1)]
    return out


def per_device(tokens, proj_in, proj_out, expert_up, expert_down, expert_ids, weight_codes):
    n_ep, n_grp = lax.axis_size("ep"), lax.axis_size("grp")
    ep, grp = lax.axis_index("ep"), lax.axis_index("grp")
    experts = n_ep * n_grp
    picks = expert_ids.shape[1]
    block = tokens.shape[0] // n_grp
    width, wide = expert_up.shape[1], expert_up.shape[2]
    high, depth = proj_in.shape
    hits = block * (picks // 2) // n_grp
    cap = max(2, (4 * block * picks + 3 * experts - 1) // (3 * experts))
    slots, lines = n_grp * cap, n_grp * hits
    me = jnp.stack([ep, grp]).astype(I32)
    shape = jax.ShapeDtypeStruct

    ids = expert_ids.T
    meta_own = jnp.concatenate([ids, weight_codes.T], axis=0)
    [ranks] = call(ranks_kernel, me, [ids], [shape((n_grp, 1, block), I32)])

    steps = range(1, n_ep // 2)
    rows_near = [proj_in, hop(proj_in, "ep", 1)]
    rows_far = [hop(proj_in, "ep", 2 * k) for k in steps]

    def partial(rows):
        columns = high * len(rows)
        return call(
            functools.partial(partial_kernel, len(rows)),
            me,
            [tokens, *rows],
            [shape((block, columns), BF16)] * n_grp,
            [pltpu.VMEM((columns, depth), BF16), pltpu.VMEM((tokens.shape[0], columns), BF16)],
            flops=2 * tokens.shape[0] * columns * depth,
        )

    def swap(cut):
        return [cut[0]] + [hop(cut[k], "grp", k) for k in range(1, n_grp)]

    def choose(ranks, arrived):
        columns = arrived[0].shape[1]
        return call(dispatch_kernel, me, [ranks, *arrived], [shape((hits, columns), BF16)] * n_grp)

    cut_near = partial(rows_near)
    meta_own = after(meta_own, cut_near[0])
    arrived_near = swap(cut_near)
    rows_far = [after(part, *arrived_near) for part in rows_far]
    metas = [meta_own, hop(meta_own, "ep", 1)]
    for k in steps:
        part = after(hop(meta_own, "ep", 2 * k), *arrived_near)
        metas += [part, hop(part, "ep", 1)]
    crossed_out = [hop(after(proj_out, *rows_far), "ep", 2 * k) for k in steps]
    cut_far = partial([x for part in rows_far for x in (part, hop(part, "ep", 1))])
    chosen_near = choose(after(ranks, cut_far[0]), arrived_near)
    arrived_far, near_own = swap(cut_far), jnp.concatenate(swap(chosen_near), axis=0)
    near = [near_own, hop(near_own, "ep", 1)]
    crossed_near = [hop(near_own, "ep", 2 * k) for k in steps]
    line_slot, line_weight = call(
        functools.partial(route_kernel, n_grp, picks, cap),
        after(me, chosen_near[0]),
        metas,
        [shape((n_ep, 1, lines), I32), shape((n_ep, 1, lines), F32)],
        room=3 * n_ep,
    )
    chosen_far = choose(after(ranks, near_own, line_slot, *crossed_out), arrived_far)
    far_own = jnp.concatenate(swap(chosen_far), axis=0)
    crossed_side = [hop(part, "ep", 1) for part in crossed_near]
    far = [far_own, hop(far_own, "ep", 1)]
    crossed_far = [hop(far_own, "ep", 2 * k) for k in steps]

    def up(sources, *deps):
        n = len(sources) * slots
        return call(
            functools.partial(up_kernel, sources, slots, 512),
            me,
            [after(line_slot, *deps), *[near[r] for r in sources], *[far[r] for r in sources], expert_up[0]],
            [shape((n, wide), BF16)],
            [pltpu.VMEM((n, width), BF16)],
            flops=2 * n * width * wide,
        )[0]

    def down(sources, hidden, first, stride, *deps, hides=1):
        n = len(sources) * slots
        return call(
            functools.partial(down_kernel, sources, slots, width // 2, first, stride),
            me,
            [after(line_slot, *deps), line_weight, hidden, expert_down[0]],
            [shape((lines, width), BF16)] * len(sources),
            [pltpu.VMEM((n, wide), BF16), pltpu.VMEM((n, width), BF16)],
            flops=hides * 2 * n * width * wide,
        )

    here, there = list(range(2)), list(range(2, n_ep))
    hidden_here = up(here, *crossed_side)
    local = down(here, hidden_here, 0, 1)
    crossed_far = [after(part, *local) for part in crossed_far]
    local = [local[0], hop(local[1], "ep", 1)]
    for k in steps:
        near += [crossed_near[k - 1], crossed_side[k - 1]]
        far += [crossed_far[k - 1], hop(crossed_far[k - 1], "ep", 1)]
    hidden_there = up(there)
    rows_out = [proj_out, hop(proj_out, "ep", 1)]
    for part in crossed_out:
        rows_out += [part, hop(part, "ep", 1)]
    odd = down(there[1::2], hidden_there, 1, 2)
    other = [hop(part, "ep", 1) for part in odd]
    even = down(there[::2], hidden_there, 0, 2, *odd)
    sums = call(add_kernel, me, [*even, *other], [shape((lines, width // 2), BF16)] * (2 * len(even)))
    half = width // 2
    returned = [[hop(sums[2 * k + h], "ep", 2 * k + 2) for k in range(len(even))] for h in range(2)]
    [rows_out] = call(rows_kernel, me, rows_out, [shape((width, depth), BF16)])

    def join(h, arrived):
        parts = [*local, *returned[h]]
        kernel = functools.partial(join_kernel, len(parts), h)
        return call(kernel, after(me, *arrived), parts, [shape((hits, half), BF16)] * n_grp)

    def combine(arrived):
        return call(combine_kernel, me, [ranks, *arrived], [shape((block, half), BF16)])[0]

    def gather(latent_out):
        blocks = [latent_out]
        for k in range(1, n_grp):
            low = k & -k
            blocks.append(hop(blocks[k ^ low], "grp", low))
        return blocks

    def mix(h, blocks, total):
        return call(
            functools.partial(mixed_kernel, h),
            me,
            [rows_out, *blocks, *total],
            [shape((tokens.shape[0], depth), BF16 if h else F32)],
            [pltpu.VMEM((tokens.shape[0], half), BF16)],
            flops=2 * tokens.shape[0] * half * depth,
        )

    arrived = swap(join(0, ()))
    latent_out = combine(arrived)
    cut = join(1, (latent_out,))
    total = mix(0, gather(latent_out), ())
    return mix(1, gather(combine(swap(cut))), total)[0]


def solution(mesh):
    in_specs = (
        P(("rep", "ep"), "grp"),
        P("ep", "grp"),
        P("ep", "grp"),
        P(("ep", "grp"), None, None),
        P(("ep", "grp"), None, None),
        P(("rep", "ep"), None),
        P(("rep", "ep"), None),
    )
    out_specs = P(("rep", "ep"), "grp")
    return jax.shard_map(
        per_device, mesh=mesh, in_specs=in_specs, out_specs=out_specs, check_vma=False
    )
```

```python
import functools
import math

import jax
import jax.numpy as jnp
from jax import lax
from jax.experimental import pallas as pl
from jax.experimental.pallas import tpu as pltpu
from jax.sharding import PartitionSpec as P

BF16, F32, I32 = jnp.bfloat16, jnp.float32, jnp.int32


def hop(x, axis, step):
    count = lax.axis_size(axis)
    return lax.ppermute(x, axis, [(i, i ^ step) for i in range(count)])


def after(x, *earlier):
    return lax.optimization_barrier((x, *earlier))[0]


def call(kernel, me, operands, outs, scratch=(), flops=1, room=4, told=True):
    vmem = pl.BlockSpec(memory_space=pltpu.VMEM)
    def size(arrays):
        return sum(math.prod(x.shape) * jnp.dtype(x.dtype).itemsize for x in arrays)

    moved = size(operands) + size(outs)
    limit = min(56 * 2**20, moved + size(scratch) + room * 2**20)
    return pl.pallas_call(
        kernel,
        out_shape=tuple(outs),
        in_specs=[pl.BlockSpec(memory_space=pltpu.SMEM)] + [vmem] * len(operands),
        out_specs=tuple(vmem for _ in outs),
        scratch_shapes=list(scratch),
        cost_estimate=pl.CostEstimate(
            flops=flops if told else 1, bytes_accessed=moved if told else 1, transcendentals=0
        ),
        compiler_params=pltpu.CompilerParams(vmem_limit_bytes=limit),
    )(me, *operands)


def partial_kernel(n_rows, me_ref, tokens_ref, *refs):
    rows, outs, (kept_ref, weights, product) = refs[:n_rows], refs[n_rows:-3], refs[-3:]
    n_blocks = len(outs)
    high = rows[0].shape[0]
    core, grp = me_ref[0] & 1, me_ref[1]
    for q in range(n_rows):
        place = pl.multiple_of((q // 2) * 2 * high + (core ^ (q % 2)) * high, high)
        weights[pl.ds(place, high), :] = rows[q][...]
    tile = min(256, product.shape[1])
    for start in range(0, product.shape[1], tile):
        product[:, start : start + tile] = lax.dot_general(
            tokens_ref[...], weights[start : start + tile, :], (((1,), (1,)), ((), ())), preferred_element_type=F32
        ).astype(BF16)
    kept_ref[...] = tokens_ref[: kept_ref.shape[0], :]
    block = product.shape[0] // n_blocks
    for k, out in enumerate(outs):
        out[...] = product[pl.ds(pl.multiple_of((grp ^ k) * block, block), block), :]


def one_hot(codes, height):
    at = lax.broadcasted_iota(I32, (height, codes.shape[1]), 0)
    return jnp.where(at == codes, 1.0, 0.0).astype(BF16)


def earlier(hits):
    n = hits.shape[1]
    before = lax.broadcasted_iota(I32, (n, n), 0) < lax.broadcasted_iota(I32, (n, n), 1)
    return jnp.dot(hits.astype(BF16), jnp.where(before, 1.0, 0.0).astype(BF16), preferred_element_type=F32)


def ranks_kernel(me_ref, ids_ref, out_ref):
    groups = out_ref.shape[0]
    block = out_ref.shape[2]
    ids = ids_ref[:, pl.ds(pl.multiple_of(me_ref[1] * block, block), block)] & (groups - 1)
    hits = jnp.concatenate(
        [jnp.max(jnp.where(ids == (me_ref[1] ^ k), 1.0, 0.0), axis=0, keepdims=True) for k in range(groups)], axis=0
    )
    ranks = jnp.where(hits > 0.0, earlier(hits), -1.0).astype(I32)
    for k in range(groups):
        out_ref[k] = ranks[k : k + 1, :]


def route_kernel(groups, picks, cap, me_ref, *refs):
    metas, slot_ref, weight_ref = refs[:-2], refs[-2], refs[-1]
    block = metas[0].shape[1] // groups
    lines = slot_ref.shape[2]
    hits, picked, weights = [], [], []
    expert = me_ref[0] * groups + me_ref[1]
    for meta in metas:
        for k in range(groups):
            place = pl.ds(pl.multiple_of((me_ref[1] ^ k) * block, block), block)
            ids, codes = meta[:picks, place], meta[picks:, place].astype(F32)
            mine = jnp.where(ids == expert, 1.0, 0.0)
            hits.append(jnp.max(jnp.where((ids & (groups - 1)) == me_ref[1], 1.0, 0.0), axis=0, keepdims=True))
            picked.append(jnp.max(mine, axis=0, keepdims=True))
            weights.append(
                jnp.sum(mine * codes, axis=0, keepdims=True) / jnp.sum(codes, axis=0, keepdims=True)
            )
    ranks = earlier(jnp.concatenate(hits, axis=0))
    slots = earlier(jnp.concatenate(picked, axis=0))
    for r in range(len(metas)):
        rows = range(r * groups, (r + 1) * groups)
        height = lines // groups
        line = jnp.concatenate(
            [jnp.where(hits[i] > 0.0, ranks[i : i + 1, :] + k * height, -1.0) for k, i in enumerate(rows)], axis=1
        ).astype(I32)
        slot = jnp.concatenate(
            [jnp.where(picked[i] > 0.0, slots[i : i + 1, :] + (k * cap + 1), 0.0) for k, i in enumerate(rows)], axis=1
        )
        weight = jnp.concatenate([weights[i] for i in rows], axis=1)
        at = jnp.where(lax.broadcasted_iota(I32, (lines, line.shape[1]), 0) == line, 1.0, 0.0)
        moved = lax.dot_general(
            jnp.concatenate([slot, weight], axis=0), at, (((1,), (1,)), ((), ())),
            precision=lax.Precision.HIGHEST, preferred_element_type=F32,
        )
        slot_ref[r] = moved[:1, :].astype(I32) - 1
        weight_ref[r] = moved[1:, :]


def dispatch_kernel(me_ref, ranks_ref, *refs):
    n = len(refs) // 2
    parts, outs = refs[:n], refs[n:]
    total = parts[0][...].astype(F32)
    for part in parts[1:]:
        total += part[...].astype(F32)
    latent = total.astype(BF16)
    for k, out in enumerate(outs):
        pick = one_hot(ranks_ref[k], out.shape[0])
        out[...] = jnp.dot(pick, latent, preferred_element_type=F32).astype(BF16)


def up_kernel(sources, slots, tile, me_ref, slot_ref, *refs):
    n = len(sources)
    near, far, (up_ref, hidden_ref, placed) = refs[:n], refs[n : 2 * n], refs[2 * n :]
    pair = near[0].shape[1]
    chip = me_ref[0] // 2
    for i, r in enumerate(sources):
        pick = one_hot(slot_ref[r], slots)
        for j in range(up_ref.shape[0] // pair):
            part = near[i][...] if j == 0 else far[i][:, (j - 1) * pair : j * pair]
            column = pl.multiple_of((chip ^ (r // 2) ^ j) * pair, pair)
            placed[i * slots : (i + 1) * slots, pl.ds(column, pair)] = jnp.dot(
                pick, part, preferred_element_type=F32
            ).astype(BF16)
    total = hidden_ref.shape[1]
    for start in range(0, total, tile):
        span = slice(start, min(start + tile, total))
        hidden = jnp.dot(placed[...], up_ref[:, span], preferred_element_type=F32)
        hidden_ref[:, span] = jnp.square(jnp.maximum(hidden, 0.0)).astype(BF16)


def down_kernel(sources, slots, tile, first, stride, me_ref, slot_ref, weight_ref, hidden_ref, down_ref, *refs):
    outs, picked, scaled = refs[:-2], refs[-2], refs[-1]
    picks = [one_hot(slot_ref[r], slots) for r in sources]
    scale = jnp.concatenate(
        [jnp.sum(pick.astype(F32) * weight_ref[r], axis=1, keepdims=True) for pick, r in zip(picks, sources)], axis=0
    )
    for i in range(len(sources)):
        at = (first + i * stride) * slots
        picked[i * slots : (i + 1) * slots, :] = hidden_ref[at : at + slots, :]
    for start in range(0, scaled.shape[1], tile):
        span = slice(start, start + tile)
        result = jnp.dot(picked[...], down_ref[:, span], preferred_element_type=F32)
        scaled[:, span] = (result * scale).astype(BF16)
        for i, out in enumerate(outs):
            out[:, span] = lax.dot_general(
                picks[i], scaled[i * slots : (i + 1) * slots, span], (((0,), (0,)), ((), ())), preferred_element_type=F32
            ).astype(BF16)


def add_kernel(me_ref, *refs):
    n = len(refs) // 4
    half = refs[0].shape[1] // 2
    for i in range(n):
        for h in range(2):
            span = slice(h * half, (h + 1) * half)
            refs[2 * n + 2 * i + h][...] = (
                refs[i][:, span].astype(F32) + refs[n + i][:, span].astype(F32)
            ).astype(BF16)


def join_kernel(n_in, h, me_ref, *refs):
    parts, outs = refs[:n_in], refs[n_in:]
    height, width = outs[0].shape
    for k, out in enumerate(outs):
        rows = slice(k * height, (k + 1) * height)
        total = jnp.zeros((height, width), F32)
        for part in parts:
            first = h * width if part.shape[1] > width else 0
            total += part[rows, first : first + width].astype(F32)
        out[...] = total.astype(BF16)


def combine_kernel(me_ref, ranks_ref, *refs):
    parts, out = refs[:-1], refs[-1]
    total = jnp.zeros(out.shape, F32)
    for k, part in enumerate(parts):
        pick = one_hot(ranks_ref[k], part.shape[0])
        total += lax.dot_general(pick, part[...], (((0,), (0,)), ((), ())), preferred_element_type=F32)
    out[...] = total.astype(BF16)


def rows_kernel(me_ref, *refs):
    rows, out_ref = refs[:-1], refs[-1]
    high = rows[0].shape[0]
    for q, row in enumerate(rows):
        out_ref[pl.ds(pl.multiple_of((me_ref[0] ^ q) * high, high), high), :] = row[...]


def mixed_kernel(h, me_ref, weights_ref, *refs):
    latents, out_ref, gathered = refs[: -2 - h], refs[-2], refs[-1]
    block, width = latents[0].shape
    for k, part in enumerate(latents):
        gathered[pl.ds(pl.multiple_of((me_ref[1] ^ k) * block, block), block), :] = part[...]
    tile = min(256, out_ref.shape[1])
    for start in range(0, out_ref.shape[1], tile):
        span = slice(start, start + tile)
        total = jnp.dot(
            gathered[...], weights_ref[h * width : (h + 1) * width, span], preferred_element_type=F32
        )
        if h:
            total += refs[-3][:, span]
        out_ref[:, span] = total.astype(out_ref.dtype)


def spread_ep(x):
    count = lax.axis_size("ep")
    near = [x] + [hop(x, "ep", 2 * k) for k in range(1, count // 2)]
    out = []
    for part in near:
        out += [part, hop(part, "ep", 1)]
    return out


def per_device(tokens, proj_in, proj_out, expert_up, expert_down, expert_ids, weight_codes):
    n_ep, n_grp = lax.axis_size("ep"), lax.axis_size("grp")
    ep, grp = lax.axis_index("ep"), lax.axis_index("grp")
    experts = n_ep * n_grp
    picks = expert_ids.shape[1]
    block = tokens.shape[0] // n_grp
    width, wide = expert_up.shape[1], expert_up.shape[2]
    high, depth = proj_in.shape
    hits = block * (picks // 2) // n_grp
    cap = max(2, (4 * block * picks + 3 * experts - 1) // (3 * experts))
    slots, lines = n_grp * cap, n_grp * hits
    me = jnp.stack([ep, grp]).astype(I32)
    shape = jax.ShapeDtypeStruct

    ids = expert_ids.T
    meta_own = jnp.concatenate([ids, weight_codes.T], axis=0)
    [ranks] = call(ranks_kernel, me, [ids], [shape((n_grp, 1, block), I32)])

    steps = range(1, n_ep // 2)
    rows_near = [proj_in, hop(proj_in, "ep", 1)]
    rows_far = [hop(proj_in, "ep", 2 * k) for k in steps]

    def partial(tokens, rows, kept):
        columns = high * len(rows)
        *cut, again = call(
            functools.partial(partial_kernel, len(rows)),
            me,
            [tokens, *rows],
            [shape((block, columns), BF16)] * n_grp + [shape((kept, depth), BF16)],
            [pltpu.VMEM((columns, depth), BF16), pltpu.VMEM((tokens.shape[0], columns), BF16)],
            flops=2 * tokens.shape[0] * columns * depth,
        )
        return cut, again

    def swap(cut):
        return [cut[0]] + [hop(cut[k], "grp", k) for k in range(1, n_grp)]

    def choose(ranks, arrived):
        columns = arrived[0].shape[1]
        return call(dispatch_kernel, me, [ranks, *arrived], [shape((hits, columns), BF16)] * n_grp)

    cut_near, kept = partial(tokens, rows_near, tokens.shape[0])
    meta_own = after(meta_own, cut_near[0])
    arrived_near = swap(cut_near)
    metas = [meta_own, hop(meta_own, "ep", 1)]
    meta_far = [hop(meta_own, "ep", 2 * k) for k in steps]
    for part in meta_far:
        metas += [part, hop(part, "ep", 1)]
    line_slot, line_weight = call(
        functools.partial(route_kernel, n_grp, picks, cap),
        me,
        metas,
        [shape((n_ep, 1, lines), I32), shape((n_ep, 1, lines), F32)],
        room=3 * n_ep,
    )
    rows_far = [after(part, *arrived_near, ranks, line_slot) for part in rows_far]
    cut_far, _ = partial(kept, [x for part in rows_far for x in (part, hop(part, "ep", 1))], 16)
    chosen_near = choose(ranks, arrived_near)
    arrived_far, pieces = swap(cut_far), swap(chosen_near)
    pieces = lax.optimization_barrier((*pieces, *arrived_far))[:n_grp]
    near_own = jnp.concatenate(pieces, axis=0)
    rows_out = [proj_out, hop(proj_out, "ep", 1)]
    for k in steps:
        part = hop(after(proj_out, *rows_far), "ep", 2 * k)
        rows_out += [part, hop(part, "ep", 1)]
    [rows_out] = call(rows_kernel, me, rows_out, [shape((width, depth), BF16)])
    near = [near_own, hop(near_own, "ep", 1)]
    crossed_near = [hop(near_own, "ep", 2 * k) for k in steps]
    chosen_far = choose(after(ranks, pieces[0], rows_out), arrived_far)
    far_own = jnp.concatenate(swap(chosen_far), axis=0)
    crossed_side = [hop(part, "ep", 1) for part in crossed_near]
    far = [far_own, hop(far_own, "ep", 1)]
    crossed_far = [hop(far_own, "ep", 2 * k) for k in steps]

    def up(sources, *deps, told=True):
        n = len(sources) * slots
        return call(
            functools.partial(up_kernel, sources, slots, 512),
            me,
            [after(line_slot, *deps), *[near[r] for r in sources], *[far[r] for r in sources], expert_up[0]],
            [shape((n, wide), BF16)],
            [pltpu.VMEM((n, width), BF16)],
            flops=2 * n * width * wide,
            told=told,
        )[0]

    def down(sources, hidden, first, stride, *deps, told=True):
        n = len(sources) * slots
        return call(
            functools.partial(down_kernel, sources, slots, width // 2, first, stride),
            me,
            [after(line_slot, *deps), line_weight, hidden, expert_down[0]],
            [shape((lines, width), BF16)] * len(sources),
            [pltpu.VMEM((n, wide), BF16), pltpu.VMEM((n, width), BF16)],
            flops=2 * n * width * wide,
            told=told,
        )

    here, there = list(range(2)), list(range(2, n_ep))
    hidden_here = up(here, *crossed_side)
    local = down(here, hidden_here, 0, 1)
    crossed_far = [after(part, *local) for part in crossed_far]
    local = [local[0], hop(local[1], "ep", 1)]
    for k in steps:
        near += [crossed_near[k - 1], crossed_side[k - 1]]
        far += [crossed_far[k - 1], hop(crossed_far[k - 1], "ep", 1)]
    hidden_there = up(there, told=False)
    odd = down(there[1::2], hidden_there, 1, 2, told=False)
    other = [hop(part, "ep", 1) for part in odd]
    even = down(there[::2], hidden_there, 0, 2, *odd, told=False)
    sums = call(add_kernel, me, [*even, *other], [shape((lines, width // 2), BF16)] * (2 * len(even)))
    half = width // 2
    returned = [[hop(sums[2 * k + h], "ep", 2 * k + 2) for k in range(len(even))] for h in range(2)]

    def join(h, arrived):
        parts = [*local, *returned[h]]
        kernel = functools.partial(join_kernel, len(parts), h)
        return call(kernel, after(me, *arrived), parts, [shape((hits, half), BF16)] * n_grp)

    def combine(ranks, arrived):
        return call(combine_kernel, me, [ranks, *arrived], [shape((block, half), BF16)])[0]

    def gather(latent_out):
        blocks = [latent_out]
        for k in range(1, n_grp):
            low = k & -k
            blocks.append(hop(blocks[k ^ low], "grp", low))
        return blocks

    def mix(h, blocks, total):
        return call(
            functools.partial(mixed_kernel, h),
            me,
            [rows_out, *blocks, *total],
            [shape((tokens.shape[0], depth), BF16 if h else F32)],
            [pltpu.VMEM((tokens.shape[0], half), BF16)],
            flops=2 * tokens.shape[0] * half * depth,
        )

    arrived = swap(join(0, ()))
    cut = join(1, arrived[1:2])
    latent_out = combine(after(ranks, cut[0]), arrived)
    first = gather(latent_out)
    ranks = after(ranks, *(first[1 << i] for i in range(n_grp.bit_length() - 1)))
    second = gather(combine(ranks, swap(cut)))
    return mix(1, second, mix(0, first, ()))[0]


def solution(mesh):
    in_specs = (
        P(("rep", "ep"), "grp"),
        P("ep", "grp"),
        P("ep", "grp"),
        P(("ep", "grp"), None, None),
        P(("ep", "grp"), None, None),
        P(("rep", "ep"), None),
        P(("rep", "ep"), None),
    )
    out_specs = P(("rep", "ep"), "grp")
    return jax.shard_map(
        per_device, mesh=mesh, in_specs=in_specs, out_specs=out_specs, check_vma=False
    )
```

```python
import functools
import math

import jax
import jax.numpy as jnp
from jax import lax
from jax.experimental import pallas as pl
from jax.experimental.pallas import tpu as pltpu
from jax.sharding import PartitionSpec as P

BF16, F32, I32 = jnp.bfloat16, jnp.float32, jnp.int32


def hop(x, axis, step):
    count = lax.axis_size(axis)
    return lax.ppermute(x, axis, [(i, i ^ step) for i in range(count)])


def after(x, *earlier):
    return lax.optimization_barrier((x, *earlier))[0]


def call(kernel, me, operands, outs, scratch=(), flops=1, room=4, told=True):
    vmem = pl.BlockSpec(memory_space=pltpu.VMEM)
    def size(arrays):
        return sum(math.prod(x.shape) * jnp.dtype(x.dtype).itemsize for x in arrays)

    moved = size(operands) + size(outs)
    limit = min(56 * 2**20, moved + size(scratch) + room * 2**20)
    return pl.pallas_call(
        kernel,
        out_shape=tuple(outs),
        in_specs=[pl.BlockSpec(memory_space=pltpu.SMEM)] + [vmem] * len(operands),
        out_specs=tuple(vmem for _ in outs),
        scratch_shapes=list(scratch),
        cost_estimate=pl.CostEstimate(
            flops=flops if told else 1, bytes_accessed=moved if told else 1, transcendentals=0
        ),
        compiler_params=pltpu.CompilerParams(vmem_limit_bytes=limit),
    )(me, *operands)


def partial_kernel(n_rows, me_ref, tokens_ref, *refs):
    rows, outs, (kept_ref, weights, product) = refs[:n_rows], refs[n_rows:-3], refs[-3:]
    n_blocks = len(outs)
    high = rows[0].shape[0]
    core, grp = me_ref[0] & 1, me_ref[1]
    for q in range(n_rows):
        place = pl.multiple_of((q // 2) * 2 * high + (core ^ (q % 2)) * high, high)
        weights[pl.ds(place, high), :] = rows[q][...]
    tile = min(256, product.shape[1])
    for start in range(0, product.shape[1], tile):
        product[:, start : start + tile] = lax.dot_general(
            tokens_ref[...], weights[start : start + tile, :], (((1,), (1,)), ((), ())), preferred_element_type=F32
        ).astype(BF16)
    kept_ref[...] = tokens_ref[: kept_ref.shape[0], :]
    block = product.shape[0] // n_blocks
    for k, out in enumerate(outs):
        out[...] = product[pl.ds(pl.multiple_of((grp ^ k) * block, block), block), :]


def one_hot(codes, height):
    at = lax.broadcasted_iota(I32, (height, codes.shape[1]), 0)
    return jnp.where(at == codes, 1.0, 0.0).astype(BF16)


def earlier(hits):
    n = hits.shape[1]
    before = lax.broadcasted_iota(I32, (n, n), 0) < lax.broadcasted_iota(I32, (n, n), 1)
    return jnp.dot(hits.astype(BF16), jnp.where(before, 1.0, 0.0).astype(BF16), preferred_element_type=F32)


def ranks_kernel(me_ref, ids_ref, out_ref):
    groups = out_ref.shape[0]
    block = out_ref.shape[2]
    ids = ids_ref[:, pl.ds(pl.multiple_of(me_ref[1] * block, block), block)] & (groups - 1)
    hits = jnp.concatenate(
        [jnp.max(jnp.where(ids == (me_ref[1] ^ k), 1.0, 0.0), axis=0, keepdims=True) for k in range(groups)], axis=0
    )
    ranks = jnp.where(hits > 0.0, earlier(hits), -1.0).astype(I32)
    for k in range(groups):
        out_ref[k] = ranks[k : k + 1, :]


def route_kernel(groups, picks, cap, me_ref, *refs):
    metas, slot_ref, weight_ref = refs[:-2], refs[-2], refs[-1]
    block = metas[0].shape[1] // groups
    lines = slot_ref.shape[2]
    hits, picked, weights = [], [], []
    expert = me_ref[0] * groups + me_ref[1]
    for meta in metas:
        for k in range(groups):
            place = pl.ds(pl.multiple_of((me_ref[1] ^ k) * block, block), block)
            ids, codes = meta[:picks, place], meta[picks:, place].astype(F32)
            mine = jnp.where(ids == expert, 1.0, 0.0)
            hits.append(jnp.max(jnp.where((ids & (groups - 1)) == me_ref[1], 1.0, 0.0), axis=0, keepdims=True))
            picked.append(jnp.max(mine, axis=0, keepdims=True))
            weights.append(
                jnp.sum(mine * codes, axis=0, keepdims=True) / jnp.sum(codes, axis=0, keepdims=True)
            )
    ranks = earlier(jnp.concatenate(hits, axis=0))
    slots = earlier(jnp.concatenate(picked, axis=0))
    for r in range(len(metas)):
        rows = range(r * groups, (r + 1) * groups)
        height = lines // groups
        line = jnp.concatenate(
            [jnp.where(hits[i] > 0.0, ranks[i : i + 1, :] + k * height, -1.0) for k, i in enumerate(rows)], axis=1
        ).astype(I32)
        slot = jnp.concatenate(
            [jnp.where(picked[i] > 0.0, slots[i : i + 1, :] + (k * cap + 1), 0.0) for k, i in enumerate(rows)], axis=1
        )
        weight = jnp.concatenate([weights[i] for i in rows], axis=1)
        at = jnp.where(lax.broadcasted_iota(I32, (lines, line.shape[1]), 0) == line, 1.0, 0.0)
        moved = lax.dot_general(
            jnp.concatenate([slot, weight], axis=0), at, (((1,), (1,)), ((), ())),
            precision=lax.Precision.HIGHEST, preferred_element_type=F32,
        )
        slot_ref[r] = moved[:1, :].astype(I32) - 1
        weight_ref[r] = moved[1:, :]


def dispatch_kernel(me_ref, ranks_ref, *refs):
    n = len(refs) // 2
    parts, outs = refs[:n], refs[n:]
    total = parts[0][...].astype(F32)
    for part in parts[1:]:
        total += part[...].astype(F32)
    latent = total.astype(BF16)
    for k, out in enumerate(outs):
        pick = one_hot(ranks_ref[k], out.shape[0])
        out[...] = jnp.dot(pick, latent, preferred_element_type=F32).astype(BF16)


def up_kernel(sources, slots, tile, me_ref, slot_ref, *refs):
    n = len(sources)
    near, far, (up_ref, hidden_ref, placed) = refs[:n], refs[n : 2 * n], refs[2 * n :]
    pair = near[0].shape[1]
    chip = me_ref[0] // 2
    for i, r in enumerate(sources):
        pick = one_hot(slot_ref[r], slots)
        for j in range(up_ref.shape[0] // pair):
            part = near[i][...] if j == 0 else far[i][:, (j - 1) * pair : j * pair]
            column = pl.multiple_of((chip ^ (r // 2) ^ j) * pair, pair)
            placed[i * slots : (i + 1) * slots, pl.ds(column, pair)] = jnp.dot(
                pick, part, preferred_element_type=F32
            ).astype(BF16)
    total = hidden_ref.shape[1]
    for start in range(0, total, tile):
        span = slice(start, min(start + tile, total))
        hidden = jnp.dot(placed[...], up_ref[:, span], preferred_element_type=F32)
        hidden_ref[:, span] = jnp.square(jnp.maximum(hidden, 0.0)).astype(BF16)


def down_kernel(sources, slots, tile, me_ref, slot_ref, weight_ref, hidden_ref, down_ref, *refs):
    outs, scaled = refs[:-1], refs[-1]
    picks = [one_hot(slot_ref[r], slots) for r in sources]
    scale = jnp.concatenate(
        [jnp.sum(pick.astype(F32) * weight_ref[r], axis=1, keepdims=True) for pick, r in zip(picks, sources)], axis=0
    )
    for start in range(0, scaled.shape[1], tile):
        span = slice(start, start + tile)
        result = jnp.dot(hidden_ref[...], down_ref[:, span], preferred_element_type=F32)
        scaled[:, span] = (result * scale).astype(BF16)
        for i, out in enumerate(outs):
            out[:, span] = lax.dot_general(
                picks[i], scaled[i * slots : (i + 1) * slots, span], (((0,), (0,)), ((), ())), preferred_element_type=F32
            ).astype(BF16)


def add_kernel(me_ref, *refs):
    n = len(refs) // 4
    half = refs[0].shape[1] // 2
    for i in range(n):
        for h in range(2):
            span = slice(h * half, (h + 1) * half)
            refs[2 * n + 2 * i + h][...] = (
                refs[i][:, span].astype(F32) + refs[n + i][:, span].astype(F32)
            ).astype(BF16)


def join_kernel(n_in, h, me_ref, *refs):
    parts, outs = refs[:n_in], refs[n_in:]
    height, width = outs[0].shape
    for k, out in enumerate(outs):
        rows = slice(k * height, (k + 1) * height)
        total = jnp.zeros((height, width), F32)
        for part in parts:
            first = h * width if part.shape[1] > width else 0
            total += part[rows, first : first + width].astype(F32)
        out[...] = total.astype(BF16)


def combine_kernel(me_ref, ranks_ref, *refs):
    parts, out = refs[:-1], refs[-1]
    total = jnp.zeros(out.shape, F32)
    for k, part in enumerate(parts):
        pick = one_hot(ranks_ref[k], part.shape[0])
        total += lax.dot_general(pick, part[...], (((0,), (0,)), ((), ())), preferred_element_type=F32)
    out[...] = total.astype(BF16)


def rows_kernel(me_ref, *refs):
    rows, out_ref = refs[:-1], refs[-1]
    high = rows[0].shape[0]
    for q, row in enumerate(rows):
        out_ref[pl.ds(pl.multiple_of((me_ref[0] ^ q) * high, high), high), :] = row[...]


def mixed_kernel(h, me_ref, weights_ref, *refs):
    latents, out_ref, gathered = refs[: -2 - h], refs[-2], refs[-1]
    block, width = latents[0].shape
    for k, part in enumerate(latents):
        gathered[pl.ds(pl.multiple_of((me_ref[1] ^ k) * block, block), block), :] = part[...]
    tile = min(256, out_ref.shape[1])
    for start in range(0, out_ref.shape[1], tile):
        span = slice(start, start + tile)
        total = jnp.dot(
            gathered[...], weights_ref[h * width : (h + 1) * width, span], preferred_element_type=F32
        )
        if h:
            total += refs[-3][:, span]
        out_ref[:, span] = total.astype(out_ref.dtype)


def spread_ep(x):
    count = lax.axis_size("ep")
    near = [x] + [hop(x, "ep", 2 * k) for k in range(1, count // 2)]
    out = []
    for part in near:
        out += [part, hop(part, "ep", 1)]
    return out


def per_device(tokens, proj_in, proj_out, expert_up, expert_down, expert_ids, weight_codes):
    n_ep, n_grp = lax.axis_size("ep"), lax.axis_size("grp")
    ep, grp = lax.axis_index("ep"), lax.axis_index("grp")
    experts = n_ep * n_grp
    picks = expert_ids.shape[1]
    block = tokens.shape[0] // n_grp
    width, wide = expert_up.shape[1], expert_up.shape[2]
    high, depth = proj_in.shape
    hits = block * (picks // 2) // n_grp
    cap = max(2, (4 * block * picks + 3 * experts - 1) // (3 * experts))
    slots, lines = n_grp * cap, n_grp * hits
    me = jnp.stack([ep, grp]).astype(I32)
    shape = jax.ShapeDtypeStruct

    ids = expert_ids.T
    meta_own = jnp.concatenate([ids, weight_codes.T], axis=0)
    [ranks] = call(ranks_kernel, me, [ids], [shape((n_grp, 1, block), I32)])

    steps = range(1, n_ep // 2)
    rows_near = [proj_in, hop(proj_in, "ep", 1)]
    rows_far = [hop(proj_in, "ep", 2 * k) for k in steps]

    def partial(tokens, rows, kept):
        columns = high * len(rows)
        *cut, again = call(
            functools.partial(partial_kernel, len(rows)),
            me,
            [tokens, *rows],
            [shape((block, columns), BF16)] * n_grp + [shape((kept, depth), BF16)],
            [pltpu.VMEM((columns, depth), BF16), pltpu.VMEM((tokens.shape[0], columns), BF16)],
            flops=2 * tokens.shape[0] * columns * depth,
        )
        return cut, again

    def swap(cut):
        far_first = [hop(cut[k], "grp", k) for k in range(n_grp - 1, 0, -1)]
        return [cut[0], *far_first[::-1]]

    def choose(ranks, arrived):
        columns = arrived[0].shape[1]
        return call(dispatch_kernel, me, [ranks, *arrived], [shape((hits, columns), BF16)] * n_grp)

    cut_near, kept = partial(tokens, rows_near, tokens.shape[0])
    meta_own = after(meta_own, cut_near[0])
    arrived_near = swap(cut_near)
    metas = [meta_own, hop(meta_own, "ep", 1)]
    meta_far = [hop(meta_own, "ep", 2 * k) for k in steps]
    for part in meta_far:
        metas += [part, hop(part, "ep", 1)]
    line_slot, line_weight = call(
        functools.partial(route_kernel, n_grp, picks, cap),
        me,
        metas,
        [shape((n_ep, 1, lines), I32), shape((n_ep, 1, lines), F32)],
        room=3 * n_ep,
    )
    rows_far = [after(part, *arrived_near, ranks, line_slot) for part in rows_far]
    cut_far, _ = partial(kept, [x for part in rows_far for x in (part, hop(part, "ep", 1))], 16)
    chosen_near = choose(ranks, arrived_near)
    arrived_far, pieces = swap(cut_far), swap(chosen_near)
    pieces = lax.optimization_barrier((*pieces, *arrived_far))[:n_grp]
    near_own = jnp.concatenate(pieces, axis=0)
    rows_out = [proj_out, hop(proj_out, "ep", 1)]
    for k in steps:
        part = hop(after(proj_out, *rows_far, chosen_near[0]), "ep", 2 * k)
        rows_out += [part, hop(part, "ep", 1)]
    [rows_out] = call(rows_kernel, me, rows_out, [shape((width, depth), BF16)])
    near = [near_own, hop(near_own, "ep", 1)]
    crossed_near = [hop(near_own, "ep", 2 * k) for k in steps]
    chosen_far = choose(after(ranks, pieces[0], rows_out), arrived_far)
    far_own = jnp.concatenate(swap(chosen_far), axis=0)
    crossed_side = [hop(part, "ep", 1) for part in crossed_near]
    far = [far_own, hop(far_own, "ep", 1)]
    crossed_far = [hop(far_own, "ep", 2 * k) for k in steps]

    def up(sources, *deps, told=True):
        n = len(sources) * slots
        return call(
            functools.partial(up_kernel, sources, slots, 512),
            me,
            [after(line_slot, *deps), *[near[r] for r in sources], *[far[r] for r in sources], expert_up[0]],
            [shape((n, wide), BF16)],
            [pltpu.VMEM((n, width), BF16)],
            flops=2 * n * width * wide,
            told=told,
        )[0]

    def down(sources, hidden, *deps, told=True):
        n = len(sources) * slots
        return call(
            functools.partial(down_kernel, sources, slots, width // 2),
            me,
            [after(line_slot, *deps), line_weight, hidden, expert_down[0]],
            [shape((lines, width), BF16)] * len(sources),
            [pltpu.VMEM((n, width), BF16)],
            flops=2 * n * width * wide,
            told=told,
        )

    here, there = list(range(2)), list(range(2, n_ep))
    hidden_here = up(here, *crossed_side)
    local = down(here, hidden_here)
    crossed_far = [after(part, *local) for part in crossed_far]
    local = [local[0], hop(local[1], "ep", 1)]
    for k in steps:
        near += [crossed_near[k - 1], crossed_side[k - 1]]
        far += [crossed_far[k - 1], hop(crossed_far[k - 1], "ep", 1)]
    hidden_even = up(there[::2])
    hidden_odd = up(there[1::2], hidden_even, told=False)
    odd = down(there[1::2], hidden_odd, told=False)
    other = [hop(part, "ep", 1) for part in odd]
    even = down(there[::2], hidden_even, *odd, told=False)
    sums = call(add_kernel, me, [*even, *other], [shape((lines, width // 2), BF16)] * (2 * len(even)))
    half = width // 2
    returned = [[hop(sums[2 * k + h], "ep", 2 * k + 2) for k in range(len(even))] for h in range(2)]

    def join(h, arrived):
        parts = [*local, *returned[h]]
        kernel = functools.partial(join_kernel, len(parts), h)
        return call(kernel, after(me, *arrived), parts, [shape((hits, half), BF16)] * n_grp)

    def combine(ranks, arrived, flops=1):
        return call(combine_kernel, me, [ranks, *arrived], [shape((block, half), BF16)], flops=flops)[0]

    def gather(latent_out):
        blocks = [latent_out]
        for k in range(1, n_grp):
            low = k & -k
            blocks.append(hop(blocks[k ^ low], "grp", low))
        return blocks

    def mix(h, blocks, total):
        return call(
            functools.partial(mixed_kernel, h),
            me,
            [rows_out, *blocks, *total],
            [shape((tokens.shape[0], depth), BF16 if h else F32)],
            [pltpu.VMEM((tokens.shape[0], half), BF16)],
            flops=2 * tokens.shape[0] * half * depth,
        )

    arrived = swap(join(0, ()))
    cut = join(1, arrived[1:2])
    latent_out = combine(after(ranks, cut[0]), arrived, flops=20 * 10**9)
    first = gather(latent_out)
    ranks = after(ranks, *(first[1 << i] for i in range(n_grp.bit_length() - 1)))
    second = gather(combine(ranks, swap(cut)))
    return mix(1, second, mix(0, first, ()))[0]


def solution(mesh):
    in_specs = (
        P(("rep", "ep"), "grp"),
        P("ep", "grp"),
        P("ep", "grp"),
        P(("ep", "grp"), None, None),
        P(("ep", "grp"), None, None),
        P(("rep", "ep"), None),
        P(("rep", "ep"), None),
    )
    out_specs = P(("rep", "ep"), "grp")
    return jax.shard_map(
        per_device, mesh=mesh, in_specs=in_specs, out_specs=out_specs, check_vma=False
    )
```

```python
import functools
import math

import jax
import jax.numpy as jnp
from jax import lax
from jax.experimental import pallas as pl
from jax.experimental.pallas import tpu as pltpu
from jax.sharding import PartitionSpec as P

BF16, F32, I32 = jnp.bfloat16, jnp.float32, jnp.int32


def hop(x, axis, step):
    count = lax.axis_size(axis)
    return lax.ppermute(x, axis, [(i, i ^ step) for i in range(count)])


def after(x, *earlier):
    return lax.optimization_barrier((x, *earlier))[0]


def call(kernel, me, operands, outs, scratch=(), flops=1, room=4, told=True):
    vmem = pl.BlockSpec(memory_space=pltpu.VMEM)
    def size(arrays):
        return sum(math.prod(x.shape) * jnp.dtype(x.dtype).itemsize for x in arrays)

    moved = size(operands) + size(outs)
    limit = min(56 * 2**20, moved + size(scratch) + room * 2**20)
    return pl.pallas_call(
        kernel,
        out_shape=tuple(outs),
        in_specs=[pl.BlockSpec(memory_space=pltpu.SMEM)] + [vmem] * len(operands),
        out_specs=tuple(vmem for _ in outs),
        scratch_shapes=list(scratch),
        cost_estimate=pl.CostEstimate(
            flops=flops if told else 1, bytes_accessed=moved if told else 1, transcendentals=0
        ),
        compiler_params=pltpu.CompilerParams(vmem_limit_bytes=limit),
    )(me, *operands)


def partial_kernel(n_rows, me_ref, tokens_ref, *refs):
    rows, outs, (kept_ref, weights, product) = refs[:n_rows], refs[n_rows:-3], refs[-3:]
    n_blocks = len(outs)
    high = rows[0].shape[0]
    core, grp = me_ref[0] & 1, me_ref[1]
    for q in range(n_rows):
        place = pl.multiple_of((q // 2) * 2 * high + (core ^ (q % 2)) * high, high)
        weights[pl.ds(place, high), :] = rows[q][...]
    tile = min(256, product.shape[1])
    for start in range(0, product.shape[1], tile):
        product[:, start : start + tile] = lax.dot_general(
            tokens_ref[...], weights[start : start + tile, :], (((1,), (1,)), ((), ())), preferred_element_type=F32
        ).astype(BF16)
    kept_ref[...] = tokens_ref[: kept_ref.shape[0], :]
    block = product.shape[0] // n_blocks
    for k, out in enumerate(outs):
        out[...] = product[pl.ds(pl.multiple_of((grp ^ k) * block, block), block), :]


def one_hot(codes, height):
    at = lax.broadcasted_iota(I32, (height, codes.shape[1]), 0)
    return jnp.where(at == codes, 1.0, 0.0).astype(BF16)


def earlier(hits):
    n = hits.shape[1]
    before = lax.broadcasted_iota(I32, (n, n), 0) < lax.broadcasted_iota(I32, (n, n), 1)
    return jnp.dot(hits.astype(BF16), jnp.where(before, 1.0, 0.0).astype(BF16), preferred_element_type=F32)


def ranks_kernel(me_ref, ids_ref, out_ref):
    groups = out_ref.shape[0]
    block = out_ref.shape[2]
    ids = ids_ref[:, pl.ds(pl.multiple_of(me_ref[1] * block, block), block)] & (groups - 1)
    hits = jnp.concatenate(
        [jnp.max(jnp.where(ids == (me_ref[1] ^ k), 1.0, 0.0), axis=0, keepdims=True) for k in range(groups)], axis=0
    )
    ranks = jnp.where(hits > 0.0, earlier(hits), -1.0).astype(I32)
    for k in range(groups):
        out_ref[k] = ranks[k : k + 1, :]


def route_kernel(groups, picks, cap, me_ref, *refs):
    metas, slot_ref, weight_ref = refs[:-2], refs[-2], refs[-1]
    block = metas[0].shape[1] // groups
    lines = slot_ref.shape[2]
    hits, picked, weights = [], [], []
    expert = me_ref[0] * groups + me_ref[1]
    for meta in metas:
        for k in range(groups):
            place = pl.ds(pl.multiple_of((me_ref[1] ^ k) * block, block), block)
            ids, codes = meta[:picks, place], meta[picks:, place].astype(F32)
            mine = jnp.where(ids == expert, 1.0, 0.0)
            hits.append(jnp.max(jnp.where((ids & (groups - 1)) == me_ref[1], 1.0, 0.0), axis=0, keepdims=True))
            picked.append(jnp.max(mine, axis=0, keepdims=True))
            weights.append(
                jnp.sum(mine * codes, axis=0, keepdims=True) / jnp.sum(codes, axis=0, keepdims=True)
            )
    ranks = earlier(jnp.concatenate(hits, axis=0))
    slots = earlier(jnp.concatenate(picked, axis=0))
    for r in range(len(metas)):
        rows = range(r * groups, (r + 1) * groups)
        height = lines // groups
        line = jnp.concatenate(
            [jnp.where(hits[i] > 0.0, ranks[i : i + 1, :] + k * height, -1.0) for k, i in enumerate(rows)], axis=1
        ).astype(I32)
        slot = jnp.concatenate(
            [jnp.where(picked[i] > 0.0, slots[i : i + 1, :] + (k * cap + 1), 0.0) for k, i in enumerate(rows)], axis=1
        )
        weight = jnp.concatenate([weights[i] for i in rows], axis=1)
        high = weight.astype(BF16)
        middle = (weight - high.astype(F32)).astype(BF16)
        low = (weight - high.astype(F32) - middle.astype(F32)).astype(BF16)
        moved = lax.dot_general(
            jnp.concatenate([slot.astype(BF16), high, middle, low], axis=0),
            one_hot(line, lines),
            (((1,), (1,)), ((), ())),
            preferred_element_type=F32,
        )
        slot_ref[r] = moved[:1, :].astype(I32) - 1
        weight_ref[r] = moved[1:2, :] + (moved[2:3, :] + moved[3:4, :])


def dispatch_kernel(me_ref, ranks_ref, *refs):
    n = len(refs) // 2
    parts, outs = refs[:n], refs[n:]
    total = parts[0][...].astype(F32)
    for part in parts[1:]:
        total += part[...].astype(F32)
    latent = total.astype(BF16)
    for k, out in enumerate(outs):
        pick = one_hot(ranks_ref[k], out.shape[0])
        out[...] = jnp.dot(pick, latent, preferred_element_type=F32).astype(BF16)


def up_kernel(sources, slots, tile, me_ref, slot_ref, *refs):
    n = len(sources)
    near, far, (up_ref, hidden_ref, placed) = refs[:n], refs[n : 2 * n], refs[2 * n :]
    pair = near[0].shape[1]
    chip = me_ref[0] // 2
    for i, r in enumerate(sources):
        pick = one_hot(slot_ref[r], slots)
        for j in range(up_ref.shape[0] // pair):
            part = near[i][...] if j == 0 else far[i][:, (j - 1) * pair : j * pair]
            column = pl.multiple_of((chip ^ (r // 2) ^ j) * pair, pair)
            placed[i * slots : (i + 1) * slots, pl.ds(column, pair)] = jnp.dot(
                pick, part, preferred_element_type=F32
            ).astype(BF16)
    total = hidden_ref.shape[1]
    for start in range(0, total, tile):
        span = slice(start, min(start + tile, total))
        hidden = jnp.dot(placed[...], up_ref[:, span], preferred_element_type=F32)
        hidden_ref[:, span] = jnp.square(jnp.maximum(hidden, 0.0)).astype(BF16)


def down_kernel(sources, slots, tile, me_ref, slot_ref, weight_ref, hidden_ref, down_ref, *refs):
    outs, scaled = refs[:-1], refs[-1]
    picks = [one_hot(slot_ref[r], slots) for r in sources]
    scale = jnp.concatenate(
        [jnp.sum(pick.astype(F32) * weight_ref[r], axis=1, keepdims=True) for pick, r in zip(picks, sources)], axis=0
    )
    for start in range(0, scaled.shape[1], tile):
        span = slice(start, start + tile)
        result = jnp.dot(hidden_ref[...], down_ref[:, span], preferred_element_type=F32)
        scaled[:, span] = (result * scale).astype(BF16)
        for i, out in enumerate(outs):
            out[:, span] = lax.dot_general(
                picks[i], scaled[i * slots : (i + 1) * slots, span], (((0,), (0,)), ((), ())), preferred_element_type=F32
            ).astype(BF16)


def add_kernel(me_ref, *refs):
    n = len(refs) // 4
    half = refs[0].shape[1] // 2
    for i in range(n):
        for h in range(2):
            span = slice(h * half, (h + 1) * half)
            refs[2 * n + 2 * i + h][...] = (
                refs[i][:, span].astype(F32) + refs[n + i][:, span].astype(F32)
            ).astype(BF16)


def join_kernel(n_in, h, me_ref, *refs):
    parts, outs = refs[:n_in], refs[n_in:]
    height, width = outs[0].shape
    for k, out in enumerate(outs):
        rows = slice(k * height, (k + 1) * height)
        total = jnp.zeros((height, width), F32)
        for part in parts:
            first = h * width if part.shape[1] > width else 0
            total += part[rows, first : first + width].astype(F32)
        out[...] = total.astype(BF16)


def combine_kernel(me_ref, ranks_ref, *refs):
    parts, out = refs[:-1], refs[-1]
    total = jnp.zeros(out.shape, F32)
    for k, part in enumerate(parts):
        pick = one_hot(ranks_ref[k], part.shape[0])
        total += lax.dot_general(pick, part[...], (((0,), (0,)), ((), ())), preferred_element_type=F32)
    out[...] = total.astype(BF16)


def rows_kernel(me_ref, *refs):
    rows, out_ref = refs[:-1], refs[-1]
    high = rows[0].shape[0]
    for q, row in enumerate(rows):
        out_ref[pl.ds(pl.multiple_of((me_ref[0] ^ q) * high, high), high), :] = row[...]


def mixed_kernel(h, me_ref, weights_ref, *refs):
    latents, out_ref, gathered = refs[: -2 - h], refs[-2], refs[-1]
    block, width = latents[0].shape
    for k, part in enumerate(latents):
        gathered[pl.ds(pl.multiple_of((me_ref[1] ^ k) * block, block), block), :] = part[...]
    tile = min(256, out_ref.shape[1])
    for start in range(0, out_ref.shape[1], tile):
        span = slice(start, start + tile)
        total = jnp.dot(
            gathered[...], weights_ref[h * width : (h + 1) * width, span], preferred_element_type=F32
        )
        if h:
            total += refs[-3][:, span]
        out_ref[:, span] = total.astype(out_ref.dtype)


def spread_ep(x):
    count = lax.axis_size("ep")
    near = [x] + [hop(x, "ep", 2 * k) for k in range(1, count // 2)]
    out = []
    for part in near:
        out += [part, hop(part, "ep", 1)]
    return out


def per_device(tokens, proj_in, proj_out, expert_up, expert_down, expert_ids, weight_codes):
    n_ep, n_grp = lax.axis_size("ep"), lax.axis_size("grp")
    ep, grp = lax.axis_index("ep"), lax.axis_index("grp")
    experts = n_ep * n_grp
    picks = expert_ids.shape[1]
    block = tokens.shape[0] // n_grp
    width, wide = expert_up.shape[1], expert_up.shape[2]
    high, depth = proj_in.shape
    hits = block * (picks // 2) // n_grp
    cap = max(2, (4 * block * picks + 3 * experts - 1) // (3 * experts))
    slots, lines = n_grp * cap, n_grp * hits
    me = jnp.stack([ep, grp]).astype(I32)
    shape = jax.ShapeDtypeStruct

    ids = expert_ids.T
    meta_own = jnp.concatenate([ids, weight_codes.T], axis=0)
    [ranks] = call(ranks_kernel, me, [ids], [shape((n_grp, 1, block), I32)])

    steps = range(1, n_ep // 2)
    rows_near = [proj_in, hop(proj_in, "ep", 1)]
    rows_far = [hop(proj_in, "ep", 2 * k) for k in steps]

    def partial(tokens, rows, kept):
        columns = high * len(rows)
        *cut, again = call(
            functools.partial(partial_kernel, len(rows)),
            me,
            [tokens, *rows],
            [shape((block, columns), BF16)] * n_grp + [shape((kept, depth), BF16)],
            [pltpu.VMEM((columns, depth), BF16), pltpu.VMEM((tokens.shape[0], columns), BF16)],
            flops=2 * tokens.shape[0] * columns * depth,
        )
        return cut, again

    def swap(cut):
        far_first = [hop(cut[k], "grp", k) for k in range(n_grp - 1, 0, -1)]
        return [cut[0], *far_first[::-1]]

    def choose(ranks, arrived):
        columns = arrived[0].shape[1]
        return call(dispatch_kernel, me, [ranks, *arrived], [shape((hits, columns), BF16)] * n_grp)

    cut_near, kept = partial(tokens, rows_near, tokens.shape[0])
    meta_own = after(meta_own, cut_near[0])
    arrived_near = swap(cut_near)
    metas = [meta_own, hop(meta_own, "ep", 1)]
    meta_far = [hop(meta_own, "ep", 2 * k) for k in steps]
    for part in meta_far:
        metas += [part, hop(part, "ep", 1)]
    line_slot, line_weight = call(
        functools.partial(route_kernel, n_grp, picks, cap),
        me,
        metas,
        [shape((n_ep, 1, lines), I32), shape((n_ep, 1, lines), F32)],
        room=3 * n_ep,
    )
    rows_far = [after(part, *arrived_near, ranks, line_slot) for part in rows_far]
    cut_far, _ = partial(kept, [x for part in rows_far for x in (part, hop(part, "ep", 1))], 16)
    chosen_near = choose(ranks, arrived_near)
    arrived_far, pieces = swap(cut_far), swap(chosen_near)
    pieces = lax.optimization_barrier((*pieces, *arrived_far))[:n_grp]
    near_own = jnp.concatenate(pieces, axis=0)
    rows_out = [proj_out, hop(proj_out, "ep", 1)]
    for k in steps:
        part = hop(after(proj_out, *rows_far, chosen_near[0]), "ep", 2 * k)
        rows_out += [part, hop(part, "ep", 1)]
    [rows_out] = call(rows_kernel, me, rows_out, [shape((width, depth), BF16)])
    near = [near_own, hop(near_own, "ep", 1)]
    crossed_near = [hop(near_own, "ep", 2 * k) for k in steps]
    chosen_far = choose(after(ranks, pieces[0], rows_out), arrived_far)
    far_own = jnp.concatenate(swap(chosen_far), axis=0)
    crossed_side = [hop(part, "ep", 1) for part in crossed_near]
    far = [far_own, hop(far_own, "ep", 1)]
    crossed_far = [hop(far_own, "ep", 2 * k) for k in steps]

    def up(sources, *deps, told=True):
        n = len(sources) * slots
        return call(
            functools.partial(up_kernel, sources, slots, 512),
            me,
            [after(line_slot, *deps), *[near[r] for r in sources], *[far[r] for r in sources], expert_up[0]],
            [shape((n, wide), BF16)],
            [pltpu.VMEM((n, width), BF16)],
            flops=2 * n * width * wide,
            told=told,
        )[0]

    def down(sources, hidden, *deps, told=True):
        n = len(sources) * slots
        return call(
            functools.partial(down_kernel, sources, slots, width // 2),
            me,
            [after(line_slot, *deps), line_weight, hidden, expert_down[0]],
            [shape((lines, width), BF16)] * len(sources),
            [pltpu.VMEM((n, width), BF16)],
            flops=2 * n * width * wide,
            told=told,
        )

    here, there = list(range(2)), list(range(2, n_ep))
    hidden_here = up(here, *crossed_side)
    local = down(here, hidden_here)
    crossed_far = [after(part, *local) for part in crossed_far]
    local = [local[0], hop(local[1], "ep", 1)]
    for k in steps:
        near += [crossed_near[k - 1], crossed_side[k - 1]]
        far += [crossed_far[k - 1], hop(crossed_far[k - 1], "ep", 1)]
    hidden_even = up(there[::2])
    hidden_odd = up(there[1::2], hidden_even, told=False)
    odd = down(there[1::2], hidden_odd, told=False)
    other = [hop(part, "ep", 1) for part in odd]
    even = down(there[::2], hidden_even, *odd, told=False)
    sums = call(add_kernel, me, [*even, *other], [shape((lines, width // 2), BF16)] * (2 * len(even)))
    half = width // 2
    returned = [[hop(sums[2 * k + h], "ep", 2 * k + 2) for k in range(len(even))] for h in range(2)]

    def join(h, arrived):
        parts = [*local, *returned[h]]
        kernel = functools.partial(join_kernel, len(parts), h)
        return call(kernel, after(me, *arrived), parts, [shape((hits, half), BF16)] * n_grp)

    def combine(ranks, arrived, flops=1):
        return call(combine_kernel, me, [ranks, *arrived], [shape((block, half), BF16)], flops=flops)[0]

    def gather(latent_out):
        blocks = [latent_out]
        for k in range(1, n_grp):
            low = k & -k
            blocks.append(hop(blocks[k ^ low], "grp", low))
        return blocks

    def mix(h, blocks, total):
        return call(
            functools.partial(mixed_kernel, h),
            me,
            [rows_out, *blocks, *total],
            [shape((tokens.shape[0], depth), BF16 if h else F32)],
            [pltpu.VMEM((tokens.shape[0], half), BF16)],
            flops=2 * tokens.shape[0] * half * depth,
        )

    arrived = swap(join(0, ()))
    cut = join(1, arrived[1:2])
    latent_out = combine(after(ranks, cut[0]), arrived, flops=20 * 10**9)
    first = gather(latent_out)
    ranks = after(ranks, *(first[1 << i] for i in range(n_grp.bit_length() - 1)))
    second = gather(combine(ranks, swap(cut)))
    return mix(1, second, mix(0, first, ()))[0]


def solution(mesh):
    in_specs = (
        P(("rep", "ep"), "grp"),
        P("ep", "grp"),
        P("ep", "grp"),
        P(("ep", "grp"), None, None),
        P(("ep", "grp"), None, None),
        P(("rep", "ep"), None),
        P(("rep", "ep"), None),
    )
    out_specs = P(("rep", "ep"), "grp")
    return jax.shard_map(
        per_device, mesh=mesh, in_specs=in_specs, out_specs=out_specs, check_vma=False
    )
```

```python
import functools
import math

import jax
import jax.numpy as jnp
from jax import lax
from jax.experimental import pallas as pl
from jax.experimental.pallas import tpu as pltpu
from jax.sharding import PartitionSpec as P

BF16, F32, I32 = jnp.bfloat16, jnp.float32, jnp.int32


def hop(x, axis, step):
    count = lax.axis_size(axis)
    return lax.ppermute(x, axis, [(i, i ^ step) for i in range(count)])


def after(x, *earlier):
    return lax.optimization_barrier((x, *earlier))[0]


def call(kernel, me, operands, outs, scratch=(), flops=1, room=4, told=True):
    vmem = pl.BlockSpec(memory_space=pltpu.VMEM)
    def size(arrays):
        return sum(math.prod(x.shape) * jnp.dtype(x.dtype).itemsize for x in arrays)

    moved = size(operands) + size(outs)
    limit = min(56 * 2**20, moved + size(scratch) + room * 2**20)
    return pl.pallas_call(
        kernel,
        out_shape=tuple(outs),
        in_specs=[pl.BlockSpec(memory_space=pltpu.SMEM)] + [vmem] * len(operands),
        out_specs=tuple(vmem for _ in outs),
        scratch_shapes=list(scratch),
        cost_estimate=pl.CostEstimate(
            flops=flops if told else 1, bytes_accessed=moved if told else 1, transcendentals=0
        ),
        compiler_params=pltpu.CompilerParams(vmem_limit_bytes=limit),
    )(me, *operands)


def partial_kernel(n_rows, me_ref, tokens_ref, *refs):
    rows, outs, (kept_ref, weights, product) = refs[:n_rows], refs[n_rows:-3], refs[-3:]
    n_blocks = len(outs)
    high = rows[0].shape[0]
    core, grp = me_ref[0] & 1, me_ref[1]
    for q in range(n_rows):
        place = pl.multiple_of((q // 2) * 2 * high + (core ^ (q % 2)) * high, high)
        weights[pl.ds(place, high), :] = rows[q][...]
    tile = min(256, product.shape[1])
    for start in range(0, product.shape[1], tile):
        product[:, start : start + tile] = lax.dot_general(
            tokens_ref[...], weights[start : start + tile, :], (((1,), (1,)), ((), ())), preferred_element_type=F32
        ).astype(BF16)
    kept_ref[...] = tokens_ref[: kept_ref.shape[0], :]
    block = product.shape[0] // n_blocks
    for k, out in enumerate(outs):
        out[...] = product[pl.ds(pl.multiple_of((grp ^ k) * block, block), block), :]


def one_hot(codes, height):
    at = lax.broadcasted_iota(I32, (height, codes.shape[1]), 0)
    return jnp.where(at == codes, 1.0, 0.0).astype(BF16)


def earlier(hits):
    n = hits.shape[1]
    before = lax.broadcasted_iota(I32, (n, n), 0) < lax.broadcasted_iota(I32, (n, n), 1)
    return jnp.dot(hits.astype(BF16), jnp.where(before, 1.0, 0.0).astype(BF16), preferred_element_type=F32)


def ranks_kernel(me_ref, ids_ref, out_ref):
    groups = out_ref.shape[0]
    block = out_ref.shape[2]
    ids = ids_ref[:, pl.ds(pl.multiple_of(me_ref[1] * block, block), block)] & (groups - 1)
    hits = jnp.concatenate(
        [jnp.max(jnp.where(ids == (me_ref[1] ^ k), 1.0, 0.0), axis=0, keepdims=True) for k in range(groups)], axis=0
    )
    ranks = jnp.where(hits > 0.0, earlier(hits), -1.0).astype(I32)
    for k in range(groups):
        out_ref[k] = ranks[k : k + 1, :]


def route_kernel(groups, picks, cap, me_ref, *refs):
    metas, slot_ref, weight_ref = refs[:-2], refs[-2], refs[-1]
    block = metas[0].shape[1] // groups
    lines = slot_ref.shape[2]
    hits, picked, weights = [], [], []
    expert = me_ref[0] * groups + me_ref[1]
    for meta in metas:
        for k in range(groups):
            place = pl.ds(pl.multiple_of((me_ref[1] ^ k) * block, block), block)
            ids, codes = meta[:picks, place], meta[picks:, place].astype(F32)
            mine = jnp.where(ids == expert, 1.0, 0.0)
            hits.append(jnp.max(jnp.where((ids & (groups - 1)) == me_ref[1], 1.0, 0.0), axis=0, keepdims=True))
            picked.append(jnp.max(mine, axis=0, keepdims=True))
            weights.append(
                jnp.sum(mine * codes, axis=0, keepdims=True) / jnp.sum(codes, axis=0, keepdims=True)
            )
    ranks = earlier(jnp.concatenate(hits, axis=0))
    slots = earlier(jnp.concatenate(picked, axis=0))
    for r in range(len(metas)):
        rows = range(r * groups, (r + 1) * groups)
        height = lines // groups
        line = jnp.concatenate(
            [jnp.where(hits[i] > 0.0, ranks[i : i + 1, :] + k * height, -1.0) for k, i in enumerate(rows)], axis=1
        ).astype(I32)
        slot = jnp.concatenate(
            [jnp.where(picked[i] > 0.0, slots[i : i + 1, :] + (k * cap + 1), 0.0) for k, i in enumerate(rows)], axis=1
        )
        weight = jnp.concatenate([weights[i] for i in rows], axis=1)
        at = jnp.where(lax.broadcasted_iota(I32, (lines, line.shape[1]), 0) == line, 1.0, 0.0)
        moved = lax.dot_general(
            jnp.concatenate([slot, weight], axis=0), at, (((1,), (1,)), ((), ())),
            precision=lax.Precision.HIGHEST, preferred_element_type=F32,
        )
        slot_ref[r] = moved[:1, :].astype(I32) - 1
        weight_ref[r] = moved[1:, :]


def dispatch_kernel(me_ref, ranks_ref, *refs):
    n = len(refs) // 2
    parts, outs = refs[:n], refs[n:]
    total = parts[0][...].astype(F32)
    for part in parts[1:]:
        total += part[...].astype(F32)
    latent = total.astype(BF16)
    for k, out in enumerate(outs):
        pick = one_hot(ranks_ref[k], out.shape[0])
        out[...] = jnp.dot(pick, latent, preferred_element_type=F32).astype(BF16)


def up_kernel(sources, slots, tile, me_ref, slot_ref, *refs):
    n = len(sources)
    near, far, (up_ref, hidden_ref, placed) = refs[:n], refs[n : 2 * n], refs[2 * n :]
    pair = near[0].shape[1]
    chip = me_ref[0] // 2
    for i, r in enumerate(sources):
        pick = one_hot(slot_ref[r], slots)
        for j in range(up_ref.shape[0] // pair):
            part = near[i][...] if j == 0 else far[i][:, (j - 1) * pair : j * pair]
            column = pl.multiple_of((chip ^ (r // 2) ^ j) * pair, pair)
            placed[i * slots : (i + 1) * slots, pl.ds(column, pair)] = jnp.dot(
                pick, part, preferred_element_type=F32
            ).astype(BF16)
    total = hidden_ref.shape[1]
    for start in range(0, total, tile):
        span = slice(start, min(start + tile, total))
        hidden = jnp.dot(placed[...], up_ref[:, span], preferred_element_type=F32)
        hidden_ref[:, span] = jnp.square(jnp.maximum(hidden, 0.0)).astype(BF16)


def down_kernel(sources, slots, tile, me_ref, slot_ref, weight_ref, hidden_ref, down_ref, *refs):
    outs, scaled = refs[:-1], refs[-1]
    picks = [one_hot(slot_ref[r], slots) for r in sources]
    scale = jnp.concatenate(
        [jnp.sum(pick.astype(F32) * weight_ref[r], axis=1, keepdims=True) for pick, r in zip(picks, sources)], axis=0
    )
    for start in range(0, scaled.shape[1], tile):
        span = slice(start, start + tile)
        result = jnp.dot(hidden_ref[...], down_ref[:, span], preferred_element_type=F32)
        scaled[:, span] = (result * scale).astype(BF16)
        for i, out in enumerate(outs):
            out[:, span] = lax.dot_general(
                picks[i], scaled[i * slots : (i + 1) * slots, span], (((0,), (0,)), ((), ())), preferred_element_type=F32
            ).astype(BF16)


def add_kernel(me_ref, *refs):
    n = len(refs) // 4
    half = refs[0].shape[1] // 2
    for i in range(n):
        for h in range(2):
            span = slice(h * half, (h + 1) * half)
            refs[2 * n + 2 * i + h][...] = (
                refs[i][:, span].astype(F32) + refs[n + i][:, span].astype(F32)
            ).astype(BF16)


def join_kernel(n_in, h, me_ref, *refs):
    parts, outs = refs[:n_in], refs[n_in:]
    height, width = outs[0].shape
    for k, out in enumerate(outs):
        rows = slice(k * height, (k + 1) * height)
        total = jnp.zeros((height, width), F32)
        for part in parts:
            first = h * width if part.shape[1] > width else 0
            total += part[rows, first : first + width].astype(F32)
        out[...] = total.astype(BF16)


def combine_kernel(me_ref, ranks_ref, *refs):
    parts, out = refs[:-1], refs[-1]
    total = jnp.zeros(out.shape, F32)
    for k, part in enumerate(parts):
        pick = one_hot(ranks_ref[k], part.shape[0])
        total += lax.dot_general(pick, part[...], (((0,), (0,)), ((), ())), preferred_element_type=F32)
    out[...] = total.astype(BF16)


def rows_kernel(me_ref, *refs):
    rows, out_ref = refs[:-1], refs[-1]
    high = rows[0].shape[0]
    for q, row in enumerate(rows):
        out_ref[pl.ds(pl.multiple_of((me_ref[0] ^ q) * high, high), high), :] = row[...]


def mixed_kernel(h, me_ref, weights_ref, *refs):
    latents, out_ref, gathered = refs[: -2 - h], refs[-2], refs[-1]
    block, width = latents[0].shape
    for k, part in enumerate(latents):
        gathered[pl.ds(pl.multiple_of((me_ref[1] ^ k) * block, block), block), :] = part[...]
    tile = min(256, out_ref.shape[1])
    for start in range(0, out_ref.shape[1], tile):
        span = slice(start, start + tile)
        total = jnp.dot(
            gathered[...], weights_ref[h * width : (h + 1) * width, span], preferred_element_type=F32
        )
        if h:
            total += refs[-3][:, span]
        out_ref[:, span] = total.astype(out_ref.dtype)


def spread_ep(x):
    count = lax.axis_size("ep")
    near = [x] + [hop(x, "ep", 2 * k) for k in range(1, count // 2)]
    out = []
    for part in near:
        out += [part, hop(part, "ep", 1)]
    return out


def per_device(tokens, proj_in, proj_out, expert_up, expert_down, expert_ids, weight_codes):
    n_ep, n_grp = lax.axis_size("ep"), lax.axis_size("grp")
    ep, grp = lax.axis_index("ep"), lax.axis_index("grp")
    experts = n_ep * n_grp
    picks = expert_ids.shape[1]
    block = tokens.shape[0] // n_grp
    width, wide = expert_up.shape[1], expert_up.shape[2]
    high, depth = proj_in.shape
    hits = block * (picks // 2) // n_grp
    cap = max(2, (4 * block * picks + 3 * experts - 1) // (3 * experts))
    slots, lines = n_grp * cap, n_grp * hits
    me = jnp.stack([ep, grp]).astype(I32)
    shape = jax.ShapeDtypeStruct

    ids = expert_ids.T
    meta_own = jnp.concatenate([ids, weight_codes.T], axis=0)
    [ranks] = call(ranks_kernel, me, [ids], [shape((n_grp, 1, block), I32)])

    steps = range(1, n_ep // 2)
    rows_near = [proj_in, hop(proj_in, "ep", 1)]
    rows_far = [hop(proj_in, "ep", 2 * k) for k in steps]

    def partial(tokens, rows, kept):
        columns = high * len(rows)
        *cut, again = call(
            functools.partial(partial_kernel, len(rows)),
            me,
            [tokens, *rows],
            [shape((block, columns), BF16)] * n_grp + [shape((kept, depth), BF16)],
            [pltpu.VMEM((columns, depth), BF16), pltpu.VMEM((tokens.shape[0], columns), BF16)],
            flops=2 * tokens.shape[0] * columns * depth,
        )
        return cut, again

    def swap(cut):
        far_first = [hop(cut[k], "grp", k) for k in range(n_grp - 1, 0, -1)]
        return [cut[0], *far_first[::-1]]

    def choose(ranks, arrived):
        columns = arrived[0].shape[1]
        return call(dispatch_kernel, me, [ranks, *arrived], [shape((hits, columns), BF16)] * n_grp)

    cut_near, kept = partial(tokens, rows_near, tokens.shape[0])
    meta_own = after(meta_own, cut_near[0])
    arrived_near = swap(cut_near)
    metas = [meta_own, hop(meta_own, "ep", 1)]
    meta_far = [hop(meta_own, "ep", 2 * k) for k in steps]
    for part in meta_far:
        metas += [part, hop(part, "ep", 1)]
    line_slot, line_weight = call(
        functools.partial(route_kernel, n_grp, picks, cap),
        me,
        metas,
        [shape((n_ep, 1, lines), I32), shape((n_ep, 1, lines), F32)],
        room=3 * n_ep,
    )
    rows_far = [after(part, *arrived_near, ranks, line_slot) for part in rows_far]
    cut_far, _ = partial(kept, [x for part in rows_far for x in (part, hop(part, "ep", 1))], 16)
    chosen_near = choose(ranks, arrived_near)
    arrived_far, pieces = swap(cut_far), swap(chosen_near)
    pieces = lax.optimization_barrier((*pieces, *arrived_far))[:n_grp]
    near_own = jnp.concatenate(pieces, axis=0)
    rows_out = [proj_out, hop(proj_out, "ep", 1)]
    for k in steps:
        part = hop(after(proj_out, *rows_far, chosen_near[0]), "ep", 2 * k)
        rows_out += [part, hop(part, "ep", 1)]
    [rows_out] = call(rows_kernel, me, rows_out, [shape((width, depth), BF16)])
    near = [near_own, hop(near_own, "ep", 1)]
    crossed_near = [hop(near_own, "ep", 2 * k) for k in steps]
    chosen_far = choose(after(ranks, pieces[0], rows_out), arrived_far)
    far_own = jnp.concatenate(swap(chosen_far), axis=0)
    crossed_side = [hop(part, "ep", 1) for part in crossed_near]
    far = [far_own, hop(far_own, "ep", 1)]
    crossed_far = [hop(far_own, "ep", 2 * k) for k in steps]

    def up(sources, *deps, told=True):
        n = len(sources) * slots
        return call(
            functools.partial(up_kernel, sources, slots, 512),
            me,
            [after(line_slot, *deps), *[near[r] for r in sources], *[far[r] for r in sources], expert_up[0]],
            [shape((n, wide), BF16)],
            [pltpu.VMEM((n, width), BF16)],
            flops=2 * n * width * wide,
            told=told,
        )[0]

    def down(sources, hidden, *deps, told=True):
        n = len(sources) * slots
        return call(
            functools.partial(down_kernel, sources, slots, width // 2),
            me,
            [after(line_slot, *deps), line_weight, hidden, expert_down[0]],
            [shape((lines, width), BF16)] * len(sources),
            [pltpu.VMEM((n, width), BF16)],
            flops=2 * n * width * wide,
            told=told,
        )

    here, there = list(range(2)), list(range(2, n_ep))
    hidden_here = up(here, *crossed_side)
    local = down(here, hidden_here)
    crossed_far = [after(part, *local) for part in crossed_far]
    local = [local[0], hop(local[1], "ep", 1)]
    for k in steps:
        near += [crossed_near[k - 1], crossed_side[k - 1]]
        far += [crossed_far[k - 1], hop(crossed_far[k - 1], "ep", 1)]
    hidden_even = up(there[::2])
    hidden_odd = up(there[1::2], hidden_even, told=False)
    odd = down(there[1::2], hidden_odd, told=False)
    other = [hop(part, "ep", 1) for part in odd]
    even = down(there[::2], hidden_even, *odd, told=False)
    sums = call(add_kernel, me, [*even, *other], [shape((lines, width // 2), BF16)] * (2 * len(even)))
    half = width // 2
    returned = [[hop(sums[2 * k + h], "ep", 2 * k + 2) for k in range(len(even))] for h in range(2)]

    def join(h, arrived):
        parts = [*local, *returned[h]]
        kernel = functools.partial(join_kernel, len(parts), h)
        return call(kernel, after(me, *arrived), parts, [shape((hits, half), BF16)] * n_grp)

    def combine(ranks, arrived, flops=1):
        return call(combine_kernel, me, [ranks, *arrived], [shape((block, half), BF16)], flops=flops)[0]

    def gather(latent_out):
        blocks = [latent_out]
        for k in range(1, n_grp):
            low = k & -k
            blocks.append(hop(blocks[k ^ low], "grp", low))
        return blocks

    def mix(h, blocks, total):
        return call(
            functools.partial(mixed_kernel, h),
            me,
            [rows_out, *blocks, *total],
            [shape((tokens.shape[0], depth), BF16 if h else F32)],
            [pltpu.VMEM((tokens.shape[0], half), BF16)],
            flops=2 * tokens.shape[0] * half * depth,
        )

    arrived = swap(join(0, ()))
    cut = join(1, arrived[1:2])
    arrived_last = swap(cut)
    latent_out = combine(after(ranks, arrived_last[1]), arrived)
    first = gather(latent_out)
    ranks = after(ranks, *(first[1 << i] for i in range(n_grp.bit_length() - 1)))
    second = gather(combine(ranks, arrived_last))
    return mix(1, second, mix(0, first, ()))[0]


def solution(mesh):
    in_specs = (
        P(("rep", "ep"), "grp"),
        P("ep", "grp"),
        P("ep", "grp"),
        P(("ep", "grp"), None, None),
        P(("ep", "grp"), None, None),
        P(("rep", "ep"), None),
        P(("rep", "ep"), None),
    )
    out_specs = P(("rep", "ep"), "grp")
    return jax.shard_map(
        per_device, mesh=mesh, in_specs=in_specs, out_specs=out_specs, check_vma=False
    )
```
